128 devices in a mesh: img: 8 (over z, y_hi), txt: 16 (over y_lo, x, core).
Axes of the slice: x: 4, y: 4 (y_hi: 2, y_lo: 2; y = y_hi * 2 + y_lo), z: 4, core: 2. Of those that a mesh axis runs over, the one named last changes fastest.
Arguments:
- img_embed: bfloat16 [16384, 1152], P(('img', 'txt')), may hold values from -0.3984375 to 0.3984375
- img_tangent: bfloat16 [16384, 1152], P(('img', 'txt')), may hold values from -0.29882812 to 0.29882812
- txt_embed: bfloat16 [16384, 1152], P(('txt', 'img')), may hold values from -0.3984375 to 0.3984375
- txt_tangent: bfloat16 [16384, 1152], P(('txt', 'img')), may hold values from -0.29882812 to 0.29882812
- labels: int32 [16384], P('img'), may hold values from 0 to 16383, each once
- log_temp: float32 [1], replicated, may hold values from 1 to 2
- bias: float32 [1], replicated, may hold values from -3 to 0
- cotangent: float32 [1], replicated, may hold values from 0.05 to 0.15
Outputs:
- grad_img: float32 [16384, 1152], P(('img', 'txt'))
- grad_img_tangent: float32 [16384, 1152], P(('img', 'txt'))
- grad_txt: float32 [16384, 1152], P(('txt', 'img'))
- grad_txt_tangent: float32 [16384, 1152], P(('txt', 'img'))
The draws below stay inside these ranges and needn't reach their ends.
Inputs may be any that keep to these rules, and one draw needn't show every extreme that they name: `labels`: each text index is the positive of exactly one image row.
All inputs are finite; a program needn't handle non-finite values.
Results may differ from the reference program's by a relative error of at most 0.0032.
Values may be sent and summed in bfloat16 or wider, within the bound.
A program may use at most 128 MiB of HBM per device.

```python
import jax
import jax.numpy as jnp
from jax import lax

D = 1152
N = 16384


def steps_of(key, extent, split, smallest, largest):
    def one(axis_at, shards_of):
        heights = jax.random.uniform(jax.random.fold_in(jax.random.fold_in(key, 6), axis_at), (shards_of,), jnp.float32, smallest / len(split), largest / len(split))
        return jnp.repeat(jnp.exp(heights), extent[axis_at] // shards_of).reshape((-1,) + (1,) * (len(extent) - axis_at - 1))

    level = one(*split[0])
    for cut in split[1:]:
        level = level * one(*cut)
    return level


def scatter_about(own_key, extent, spread, reach, pieces=(), kind=jnp.bfloat16):
    drawn = spread * jax.random.normal(own_key, extent, jnp.float32)
    if pieces:
        drawn = drawn * steps_of(own_key, extent, pieces, -0.22, 0.18)
    return jnp.clip(drawn, -reach, reach).astype(kind)


def setup_inputs(seed: int = 0) -> dict:
    splits = jax.random.split(jax.random.key(seed), 9)
    return {
        "img_embed": scatter_about(splits[0], (N, D), 0.06, 0.3984375, ((0, 128),)),
        "img_tangent": scatter_about(splits[1], (N, D), 0.04, 0.29882812, ((0, 128),)),
        "txt_embed": scatter_about(splits[2], (N, D), 0.06, 0.3984375, ((0, 128),)),
        "txt_tangent": scatter_about(splits[3], (N, D), 0.04, 0.29882812, ((0, 128),)),
        "labels": jax.random.permutation(splits[4], N).astype(jnp.int32),
        "log_temp": jnp.clip(jax.random.uniform(splits[5], (1,), jnp.float32, 1.0, 2.0), 1.0, 2.0),
        "bias": jnp.clip(jax.random.uniform(splits[6], (1,), jnp.float32, -3.0, 0.0), -3.0, 0.0),
        "cotangent": jnp.clip(jax.random.uniform(splits[7], (1,), jnp.float32, 0.05, 0.15), 0.05, 0.15),
    }


def contract_rows(left, right):
    return lax.dot_general(left, right, (((0,), (0,)), ((), ())), preferred_element_type=jnp.float32)


def contract_cols(left, right):
    return lax.dot_general(left, right, (((1,), (1,)), ((), ())), preferred_element_type=jnp.float32)


def reference(img_embed, img_tangent, txt_embed, txt_tangent, labels, log_temp, bias, cotangent):
    scale = jnp.exp(log_temp[0])
    shift = bias[0]
    upstream = cotangent[0]
    img_sum = (img_embed.astype(jnp.float32) + img_tangent.astype(jnp.float32)).astype(jnp.bfloat16)
    txt_sum = (txt_embed.astype(jnp.float32) + txt_tangent.astype(jnp.float32)).astype(jnp.bfloat16)
    block = min(512, N)
    count = N // block
    width = img_embed.shape[1]
    column = jnp.arange(N, dtype=jnp.int32)
    stacked = (img_embed.reshape(count, block, width), img_tangent.reshape(count, block, width),
               img_sum.reshape(count, block, width), labels.reshape(count, block))

    def step(carry, items):
        acc_txt, acc_txt_tan = carry
        rows, rows_tan, rows_sum, row_labels = items
        logits = scale * (contract_cols(rows, txt_sum) + contract_cols(rows_tan, txt_embed)) + shift
        sign = jnp.where(row_labels[:, None] == column[None, :], 1.0, -1.0).astype(jnp.float32)
        weight = (-upstream * sign * jax.nn.sigmoid(-sign * logits)).astype(jnp.bfloat16)
        out_img = scale * jnp.dot(weight, txt_sum, preferred_element_type=jnp.float32)
        out_img_tan = scale * jnp.dot(weight, txt_embed, preferred_element_type=jnp.float32)
        acc_txt = acc_txt + scale * contract_rows(weight, rows_sum)
        acc_txt_tan = acc_txt_tan + scale * contract_rows(weight, rows)
        return (acc_txt, acc_txt_tan), (out_img, out_img_tan)

    start = (jnp.zeros((N, width), jnp.float32), jnp.zeros((N, width), jnp.float32))
    (grad_txt, grad_txt_tangent), (grad_img, grad_img_tangent) = lax.scan(step, start, stacked)
    return (grad_img.reshape(N, width), grad_img_tangent.reshape(N, width), grad_txt, grad_txt_tangent)
```

```python
import functools
import math

import jax
import jax.numpy as jnp
from jax import lax
from jax.experimental import pallas as pl
from jax.experimental.pallas import tpu as pltpu
from jax.sharding import PartitionSpec as P

MESH = pl.DeviceIdType.MESH
F32 = jnp.float32
BF16 = jnp.bfloat16
LOG2E = math.log2(math.e)

ORDER = (7, 6, 4, 3, 5, 2, 1, 0)
OWN = (0, 2, 3, 6)
KEEP0 = (0, 2, 3, 6)
KEEP1 = (0, 1, 2, 5)
TILES = ((0, 0), (0, 1), (1, 0), (1, 1),
         (2, 0), (2, 1), (0, 2), (1, 2), (2, 2),
         (3, 0), (3, 1), (3, 2), (3, 3), (2, 3), (0, 3), (1, 3))


def pick(table, index):
    value = jnp.int32(table[0])
    for at, entry in enumerate(table[1:], 1):
        value = jnp.where(index == at, jnp.int32(entry), value)
    return value


def rows_at(index, size):
    return pl.ds(pl.multiple_of(index * size, size), size)


class Copies:
    def __init__(self, send, recv):
        self.send, self.recv, self.table = send, recv, {}

    def add(self, name, src, dst, device):
        at = len(self.table)
        self.table[name] = pltpu.make_async_remote_copy(
            src_ref=src, dst_ref=dst, send_sem=self.send.at[at], recv_sem=self.recv.at[at],
            device_id=device, device_id_type=MESH)

    def start(self, *names):
        for name in names:
            self.table[name].start()

    def landed(self, *names):
        for name in names:
            self.table[name].wait_recv()

    def drain(self):
        for copy in self.table.values():
            copy.wait_send()


N_GATHER = 15 + 15 + 16
N_REDUCE = 17 + 17


def kernel(log_temp, bias, cotangent, labels, img_embed, img_tangent, txt_embed, txt_tangent,
           out_img, out_img_tan, out_txt, out_txt_tan,
           im, tx, tan, w, rel, rx_core, rx_i, rx_t, keep_i0, keep_i1, keep_t0, keep_t1,
           st_i0, st_i1, st_t0, st_t1,
           load_sem, g_send, g_recv, r_send, r_recv, c_send, c_recv):
    R, D = txt_embed.shape
    H = R // 2
    img, txt = lax.axis_index("img"), lax.axis_index("txt")
    z, y_hi = img // 2, img % 2
    y_lo, x, c = txt // 8, (txt // 2) % 4, txt % 2

    def at_txt(y_lo, x, c):
        return (y_lo * 4 + x) * 2 + c

    core = (img, at_txt(y_lo, x, 1 - c))
    i_y = (img, at_txt(1 - y_lo, x, c))
    i_p, i_m = (img, at_txt(y_lo, (x + 1) % 4, c)), (img, at_txt(y_lo, (x + 3) % 4, c))
    t_y = (z * 2 + 1 - y_hi, at_txt(1 - y_lo, x, c))
    t_p, t_m = (((z + 1) % 4) * 2 + y_hi, txt), (((z + 3) % 4) * 2 + y_hi, txt)

    loads = [
        pltpu.make_async_copy(src, dst, load_sem.at[n])
        for n, (src, dst) in enumerate((
            (img_embed, im.at[0:R, D:2 * D]), (img_tangent, im.at[0:R, 0:D]),
            (txt_embed, tx.at[0:R, 0:D]), (txt_tangent, tan)))
    ]
    for copy in loads:
        copy.start()
    barrier = pltpu.get_barrier_semaphore()
    peers = (core, i_y, i_p, i_m, t_y, t_p, t_m)
    for peer in peers:
        pl.semaphore_signal(barrier, inc=1, device_id=peer, device_id_type=MESH)
    for copy in loads:
        copy.wait()
    tx[0:R, D:2 * D] = (tx[0:R, 0:D].astype(F32) + tan[...].astype(F32)).astype(BF16)
    pl.semaphore_wait(barrier, len(peers))

    g = Copies(g_send, g_recv)
    families = (("i", im, 2 * R, D, 0, i_y, i_p, i_m), ("t", tx, R, 0, D, t_y, t_p, t_m))
    for f, buf, pitch, a, b, y, p, m in families:
        def add(name, src, dst, col, to, lo=0, hi=R, f=f, buf=buf, pitch=pitch):
            cols = slice(col, col + D)
            g.add(f + name, buf.at[src * pitch + lo:src * pitch + hi, cols],
                  buf.at[dst * pitch + lo:dst * pitch + hi, cols], to)
        add("A1", 0, 1, a, y)
        add("A3", 0, 3, a, p)
        add("A2", 0, 2, a, m)
        add("A5", 1, 5, a, p)
        add("A4", 1, 4, a, m)
        add("A6", 3, 6, a, p)
        add("A7", 4, 7, a, m)
        add("B3", 0, 3, b, p)
        add("B2", 0, 2, b, m)
        add("B6t", 3, 6, b, p, 0, H)
        add("B6b", 2, 6, b, m, H, R)
        add("B1", 0, 1, b, y)
        add("B4", 2, 4, b, y)
        add("B5", 3, 5, b, y)
        add("B7", 6, 7, b, y)
    for k in range(8):
        for name, col in (("A", D), ("B", 0)):
            g.add("c%s%d" % (name, k), im.at[2 * R * k:2 * R * k + R, col:col + D],
                  im.at[2 * R * k + R:2 * R * (k + 1), col:col + D], core)

    def both(*names):
        return [f + name for name in names for f in "it"]

    g.start(*both("A1", "A3", "A2", "B3", "B2", "B1"), "cA0", "cB0")

    lane = lax.broadcasted_iota(jnp.int32, (R, R), 1)

    def place(k, _):
        shift, other = pick((0, 0, 1, 3, 1, 3, 2, 2), k // 2), pick((0, 1, 0, 0, 1, 1, 0, 1), k // 2)
        t = at_txt(jnp.where(other == 1, 1 - y_lo, y_lo), (x + shift) % 4, jnp.where(k % 2 == 1, 1 - c, c))
        row = jnp.broadcast_to(labels[pl.ds(t, 1), :], (R, R))
        rel[rows_at(k, R), :] = row.T - lane
        return 0

    lax.fori_loop(0, 16, place, 0)

    scale = jnp.exp(jnp.full((1, R), log_temp[0], F32))
    slope, shift = scale * LOG2E, jnp.full((1, R), bias[0], F32) * LOG2E
    upstream = jnp.full((1, R), cotangent[0], F32)

    def add_up(lo, hi):
        def one(k, _):
            rows = rows_at(k, R)
            im[rows, 2 * D:3 * D] = (im[rows, 0:D].astype(F32) + im[rows, D:2 * D].astype(F32)).astype(BF16)
            return 0
        lax.fori_loop(2 * lo, 2 * hi, one, 0)

    def arrive(slots):
        for k in slots:
            g.landed("cA%d" % k, "cB%d" % k)

    def base_of(k):
        d, other = pick((0, 0, 1, 3, 1, 3, 2, 2), k), pick((0, 1, 0, 0, 1, 1, 0, 1), k)
        hi, lo = jnp.where(other == 1, 1 - y_hi, y_hi), jnp.where(other == 1, 1 - y_lo, y_lo)
        return (at_txt(lo, x, c) * 8 + ((z + d) % 4) * 2 + hi) * R

    def tile(s, _):
        @pl.when(s == 0)
        def _():
            g.landed(*both("A1"))
            g.start(*both("A5", "A4"), "cA1")
            g.landed(*both("A3", "A2"))
            g.start(*both("A6"), "cA3", "cA2")
            g.landed(*both("B3", "B2"))
            g.start(*both("B6t", "B6b", "B5", "B4"), "cB3", "cB2")
            g.landed(*both("B1"))
            g.start("cB1")
            arrive((0, 1, 2, 3))
            add_up(0, 4)

        @pl.when(s == 4)
        def _():
            g.landed(*both("A4"))
            g.start(*both("A7"), "cA4")
            g.landed(*both("B6t", "B6b"))
            g.start(*both("B7"), "cB6")
            g.landed(*both("A5"))
            g.start("cA5")
            g.landed(*both("A6"))
            g.start("cA6")
            g.landed(*both("B4", "B5"))
            g.start("cB4", "cB5")
            arrive((4, 5))
            add_up(4, 6)

        @pl.when(s == 9)
        def _():
            g.landed(*both("A7", "B7"))
            g.start("cA7", "cB7")
            arrive((6, 7))
            add_up(6, 8)

        qp, tp = pick([t[0] for t in TILES], s), pick([t[1] for t in TILES], s)
        rows, cols = rows_at(qp, 4 * R), rows_at(tp, 2 * R)
        dots = lax.dot_general(im[rows, 0:2 * D], tx[cols, :], (((1,), (1,)), ((), ())), preferred_element_type=F32)
        near = rel[rows, :]
        for half in range(2):
            logit = dots[:, half * R:(half + 1) * R] * slope + shift
            positive = near == base_of(2 * tp + half)
            power = jnp.exp2(jnp.where(positive, logit, -logit))
            weight = jnp.where(positive, -upstream, upstream) / (1.0 + power)
            w[rows, rows_at(2 * tp + half, R)] = weight.astype(BF16)
        return 0

    lax.fori_loop(0, len(TILES), tile, 0)
    g.drain()

    r = Copies(r_send, r_recv)
    reduces = (("i", rx_i, keep_i0, keep_i1, st_i0, st_i1, i_y, i_p, i_m),
               ("t", rx_t, keep_t0, keep_t1, st_t0, st_t1, t_y, t_p, t_m))
    RX = {name: n for n, name in enumerate(
        ("c1", "f1", "g1", "c2", "f2", "g2", "e1", "y0", "y2", "y3", "y6", "pm", "pp", "cc"))}
    for f, rx, _, _, s0, s1, y, p, m in reduces:
        def add(name, src, k, to, lo=0, hi=R, into=None, f=f, rx=rx):
            r.add(f + name, src.at[k, lo:hi], rx.at[RX[into or name], lo:hi], to)
        add("c2", s1, 7, m)
        add("y6", s0, 7, y)
        add("c1", s1, 6, p)
        add("g2", s1, 4, p)
        add("y2", s0, 4, y)
        add("g1", s1, 3, m)
        add("y3", s0, 5, y)
        add("y0", s0, 1, y)
        add("ct", s0, 6, p, 0, H, "cc")
        add("cb", s0, 6, m, H, R, "cc")
        add("f2", s1, 5, m)
        add("f1", s1, 2, p)
        add("pmb", s0, 2, p, H, R, "pm")
        add("pmt", s0, 2, p, 0, H, "pm")
        add("ppt", s0, 3, m, 0, H, "pp")
        add("ppb", s0, 3, m, H, R, "pp")
        add("e1", s1, 1, y)

    def core_copy(k):
        return pltpu.make_async_remote_copy(
            src_ref=im.at[rows_at(k, 2 * R), 0:D], dst_ref=rx_core.at[k],
            send_sem=c_send.at[k], recv_sem=c_recv.at[k], device_id=core, device_id_type=MESH)

    def place_of(table, k):
        value = jnp.int32(4)
        for n, entry in enumerate(table):
            value = jnp.where(k == entry, jnp.int32(n), value)
        return value

    def put(k, value0, value1, k0, k1, s0, s1):
        k0[place_of(KEEP0, k)] = value0
        k1[place_of(KEEP1, k)] = value1
        s0[k] = value0.astype(BF16)
        s1[k] = value1.astype(BF16)

    def send(k, f):
        for slot, names in ((7, ("c2", "y6")), (6, ("c1",)), (4, ("g2", "y2")), (3, ("g1",)), (5, ("y3",)), (1, ("y0",))):
            @pl.when(k == slot)
            def _(names=names):
                r.start(*[f + name for name in names])

    def events(do):
        for f, rx, k0, k1, s0, s1, *_ in reduces:
            do(f, lambda name, rx=rx: rx.at[RX[name]], k0, k1, s0, s1)

    def after_3(f, rx, k0, k1, s0, s1):
        r.landed(f + "y6")
        s0[6] = (k0[KEEP0.index(6)] + rx("y6")[...].astype(F32)).astype(BF16)
        r.start(f + "ct", f + "cb")

    def after_4(f, rx, k0, k1, s0, s1):
        r.landed(f + "c2")
        s1[5] = (k1[KEEP1.index(5)] + rx("c2")[...].astype(F32)).astype(BF16)
        r.start(f + "f2")

    def after_5(f, rx, k0, k1, s0, s1):
        r.landed(f + "c1")
        s1[2] = (k1[KEEP1.index(2)] + rx("c1")[...].astype(F32)).astype(BF16)
        r.start(f + "f1")
        r.landed(f + "y2")
        at = KEEP0.index(2)
        s0[2, H:R] = (k0[at, H:R] + rx("y2")[H:R].astype(F32)).astype(BF16)
        r.start(f + "pmb")

    def after_6(f, rx, k0, k1, s0, s1):
        r.landed(f + "ct")
        at = KEEP0.index(2)
        s0[2, 0:H] = (k0[at, 0:H] + rx("y2")[0:H].astype(F32) + rx("cc")[0:H].astype(F32)).astype(BF16)
        r.start(f + "pmt")
        r.landed(f + "y3")
        at = KEEP0.index(3)
        s0[3, 0:H] = (k0[at, 0:H] + rx("y3")[0:H].astype(F32)).astype(BF16)
        r.start(f + "ppt")
        r.landed(f + "cb")
        s0[3, H:R] = (k0[at, H:R] + rx("y3")[H:R].astype(F32) + rx("cc")[H:R].astype(F32)).astype(BF16)
        r.start(f + "ppb")

    def after_7(f, rx, k0, k1, s0, s1):
        r.landed(f + "g2", f + "f2")
        s1[1] = (k1[KEEP1.index(1)] + rx("g2")[...].astype(F32) + rx("f2")[...].astype(F32)).astype(BF16)
        r.start(f + "e1")

    def round_(n, _):
        k = pick(ORDER, n)
        give = pl.ds(pl.multiple_of(k * 2 * R + R, R), R)
        mine = pl.ds(pl.multiple_of(k * 2 * R, R), R)
        part = jnp.dot(w[give, :], tx[...], preferred_element_type=F32)
        im[mine, 0:D] = part[:, 0:D].astype(BF16)
        im[give, 0:D] = part[:, D:2 * D].astype(BF16)
        core_copy(k).start()

        part = lax.dot_general(w[:, rows_at(k, R)], im[:, D:3 * D], (((0,), (0,)), ((), ())), preferred_element_type=F32)
        put(k, part[:, 0:D], part[:, D:2 * D], keep_t0, keep_t1, st_t0, st_t1)
        send(k, "t")

        core_copy(k).wait_recv()
        part = jnp.dot(w[mine, :], tx[...], preferred_element_type=F32)
        put(k, part[:, 0:D] + rx_core[k, 0:R].astype(F32), part[:, D:2 * D] + rx_core[k, R:2 * R].astype(F32),
            keep_i0, keep_i1, st_i0, st_i1)
        send(k, "i")

        for at, do in ((3, after_3), (4, after_4), (5, after_5), (6, after_6), (7, after_7)):
            @pl.when(n == at)
            def _(do=do):
                events(do)
        return 0

    lax.fori_loop(0, 8, round_, 0)

    times = jnp.exp(jnp.full((1, D), log_temp[0], F32))
    outs = {"i": (out_img_tan, out_img), "t": (out_txt_tan, out_txt)}

    def left(f, rx, k0, k1, s0, s1):
        r.landed(f + "y0", f + "pmb", f + "pmt", f + "ppt", f + "ppb")
        outs[f][0][...] = times * (k0[0] + rx("y0")[...].astype(F32)
                                   + rx("pm")[...].astype(F32) + rx("pp")[...].astype(F32))

    def right(f, rx, k0, k1, s0, s1):
        r.landed(f + "f1", f + "g1", f + "e1")
        outs[f][1][...] = times * (k1[0] + rx("f1")[...].astype(F32)
                                   + rx("g1")[...].astype(F32) + rx("e1")[...].astype(F32))

    events(left)
    events(right)
    r.drain()
    for k in range(8):
        core_copy(k).wait_send()


def body(img_embed, img_tangent, txt_embed, txt_tangent, labels, log_temp, bias, cotangent):
    R, D = txt_embed.shape
    smem = pl.BlockSpec(memory_space=pltpu.SMEM)
    vmem = pl.BlockSpec(memory_space=pltpu.VMEM)
    anym = pl.BlockSpec(memory_space=pl.ANY)
    out = jax.ShapeDtypeStruct((R, D), F32)
    dma = pltpu.SemaphoreType.DMA
    grads = pl.pallas_call(
        kernel,
        out_shape=[out] * 4,
        in_specs=[smem] * 3 + [vmem] + [anym] * 4,
        out_specs=[vmem] * 4,
        scratch_shapes=[
            pltpu.VMEM((16 * R, 3 * D), BF16),
            pltpu.VMEM((8 * R, 2 * D), BF16),
            pltpu.VMEM((R, D), BF16),
            pltpu.VMEM((16 * R, 8 * R), BF16),
            pltpu.VMEM((16 * R, R), jnp.int32),
            pltpu.VMEM((8, 2 * R, D), BF16),
        ] + [pltpu.VMEM((14, R, D), BF16)] * 2
        + [pltpu.VMEM((5, R, D), F32)] * 4
        + [pltpu.VMEM((8, R, D), BF16)] * 4
        + [dma((4,)), dma((N_GATHER,)), dma((N_GATHER,)), dma((N_REDUCE,)), dma((N_REDUCE,)), dma((8,)), dma((8,))],
        compiler_params=pltpu.CompilerParams(
            collective_id=0, has_side_effects=True, vmem_limit_bytes=63 * 2 ** 20),
    )(log_temp, bias, cotangent, labels.reshape(16, R), img_embed, img_tangent, txt_embed, txt_tangent)
    grad_img, grad_img_tangent, grad_txt, grad_txt_tangent = grads
    return grad_img, grad_img_tangent, grad_txt, grad_txt_tangent


def solution(mesh):
    rows = P(("img", "txt"), None)
    cols = P(("txt", "img"), None)
    return jax.shard_map(
        body, mesh=mesh,
        in_specs=(rows, rows, cols, cols, P("img"), P(), P(), P()),
        out_specs=(rows, rows, cols, cols), check_vma=False)
```

```python
import functools
import math

import jax
import jax.numpy as jnp
from jax import lax
from jax.experimental import pallas as pl
from jax.experimental.pallas import tpu as pltpu
from jax.sharding import PartitionSpec as P

MESH = pl.DeviceIdType.MESH
F32 = jnp.float32
BF16 = jnp.bfloat16
LOG2E = math.log2(math.e)

ORDER = (7, 4, 6, 5, 2, 3, 1, 0)
EVENTS = (
    ("t", "y6", 4), ("t", "c2", 6), ("i", "y6", 6), ("i", "c2", 7),
    ("t", "y2", 8), ("i", "y2", 9), ("t", "e1", 12), ("t", "y3", 12),
    ("t", "cb", 12), ("t", "c1", 12), ("i", "y3", 12), ("i", "cb", 12),
    ("i", "c1", 12), ("i", "e1", 13), ("t", "ct", 13), ("i", "ct", 14),
)
KEEP0 = (0, 2, 3, 6)
KEEP1 = (0, 1, 2, 5)
TILES = ((0, 0), (0, 1), (1, 0), (1, 1),
         (2, 0), (2, 1), (0, 2), (1, 2), (2, 2),
         (3, 0), (3, 1), (3, 2), (3, 3), (2, 3), (0, 3), (1, 3))


def pick(table, index):
    value = jnp.int32(table[0])
    for at, entry in enumerate(table[1:], 1):
        value = jnp.where(index == at, jnp.int32(entry), value)
    return value


def rows_at(index, size):
    return pl.ds(pl.multiple_of(index * size, size), size)


def split(D):
    return max(1, round(2 * D * 4 / 9 / 128)) * 128


class Copies:
    def __init__(self, send, recv):
        self.send, self.recv, self.table = send, recv, {}

    def add(self, name, src, dst, device):
        at = len(self.table)
        self.table[name] = pltpu.make_async_remote_copy(
            src_ref=src, dst_ref=dst, send_sem=self.send.at[at], recv_sem=self.recv.at[at],
            device_id=device, device_id_type=MESH)

    def start(self, *names):
        for name in names:
            self.table[name].start()

    def landed(self, *names):
        for name in names:
            self.table[name].wait_recv()

    def drain(self):
        for copy in self.table.values():
            copy.wait_send()


N_GATHER = 15 + 15 + 16
N_REDUCE = 17 + 17


def kernel(log_temp_in, bias_in, cotangent_in, labels_in, img_embed, img_tangent, txt_embed, txt_tangent,
           out_img, out_img_tan, out_txt, out_txt_tan,
           im, tx, tan, w, rel, rx_core, rx_i0, rx_i1, rx_t0, rx_t1, keep_i0, keep_i1, keep_t0, keep_t1,
           st_i0, st_i1, st_t0, st_t1, log_temp, bias, cotangent, labels,
           load_sem, g_send, g_recv, r_send, r_recv, c_send, c_recv):
    R, D = txt_embed.shape
    H = R // 2
    S = split(D)
    img, txt = lax.axis_index("img"), lax.axis_index("txt")
    z, y_hi = img // 2, img % 2
    y_lo, x, c = txt // 8, (txt // 2) % 4, txt % 2

    def at_txt(y_lo, x, c):
        return (y_lo * 4 + x) * 2 + c

    core = (img, at_txt(y_lo, x, 1 - c))
    i_y = (img, at_txt(1 - y_lo, x, c))
    i_p, i_m = (img, at_txt(y_lo, (x + 1) % 4, c)), (img, at_txt(y_lo, (x + 3) % 4, c))
    t_y = (z * 2 + 1 - y_hi, at_txt(1 - y_lo, x, c))
    t_p, t_m = (((z + 1) % 4) * 2 + y_hi, txt), (((z + 3) % 4) * 2 + y_hi, txt)

    loads = [
        pltpu.make_async_copy(src, dst, load_sem.at[n])
        for n, (src, dst) in enumerate((
            (img_embed, im.at[0:R, D:2 * D]), (img_tangent, im.at[0:R, 0:D]),
            (txt_embed, tx.at[0:R, 0:D]), (txt_tangent, tan),
            (log_temp_in, log_temp), (bias_in, bias), (cotangent_in, cotangent), (labels_in, labels)))
    ]
    for copy in loads:
        copy.start()
    barrier = pltpu.get_barrier_semaphore()
    peers = (core, i_y, i_p, i_m, t_y, t_p, t_m)
    for peer in peers:
        pl.semaphore_signal(barrier, inc=1, device_id=peer, device_id_type=MESH)
    for copy in loads:
        copy.wait()
    tx[0:R, D:2 * D] = (tx[0:R, 0:D].astype(F32) + tan[...].astype(F32)).astype(BF16)
    pl.semaphore_wait(barrier, len(peers))

    g = Copies(g_send, g_recv)
    families = (("i", im, 2 * R, i_y, i_p, i_m), ("t", tx, R, t_y, t_p, t_m))
    a, b = slice(S, 2 * D), slice(0, S)
    for f, buf, pitch, y, p, m in families:
        def add(name, src, dst, col, to, lo=0, hi=R, f=f, buf=buf, pitch=pitch):
            g.add(f + name, buf.at[src * pitch + lo:src * pitch + hi, col],
                  buf.at[dst * pitch + lo:dst * pitch + hi, col], to)
        add("A1", 0, 1, a, y)
        add("A3", 0, 3, a, p)
        add("A2", 0, 2, a, m)
        add("A5", 1, 5, a, p)
        add("A4", 1, 4, a, m)
        add("A6", 3, 6, a, p)
        add("A7", 4, 7, a, m)
        add("B3", 0, 3, b, p)
        add("B2", 0, 2, b, m)
        add("B6t", 3, 6, b, p, 0, H)
        add("B6b", 2, 6, b, m, H, R)
        add("B1", 0, 1, b, y)
        add("B4", 2, 4, b, y)
        add("B5", 3, 5, b, y)
        add("B7", 6, 7, b, y)
    for k in range(8):
        for name, col in (("A", a), ("B", b)):
            g.add("c%s%d" % (name, k), im.at[2 * R * k:2 * R * k + R, col],
                  im.at[2 * R * k + R:2 * R * (k + 1), col], core)

    def both(*names):
        return [f + name for name in names for f in "it"]

    g.start(*both("A1", "B3", "B2", "A3", "A2", "B1"), "cB0", "cA0")

    lane = lax.broadcasted_iota(jnp.int32, (R, R), 1)

    def place(k, _):
        shift, other = pick((0, 0, 1, 3, 1, 3, 2, 2), k // 2), pick((0, 1, 0, 0, 1, 1, 0, 1), k // 2)
        t = at_txt(jnp.where(other == 1, 1 - y_lo, y_lo), (x + shift) % 4, jnp.where(k % 2 == 1, 1 - c, c))
        row = jnp.broadcast_to(labels[pl.ds(t, 1), :], (R, R))
        rel[rows_at(k, R), :] = row.T - lane
        return 0

    lax.fori_loop(0, 16, place, 0)

    scale = jnp.exp(jnp.broadcast_to(log_temp[...], (1, R)))
    slope, shift = scale * LOG2E, jnp.broadcast_to(bias[...], (1, R)) * LOG2E
    upstream = jnp.broadcast_to(cotangent[...], (1, R))

    def add_up(lo, hi):
        def one(k, _):
            rows = rows_at(k, R)
            im[rows, 2 * D:3 * D] = (im[rows, 0:D].astype(F32) + im[rows, D:2 * D].astype(F32)).astype(BF16)
            return 0
        lax.fori_loop(2 * lo, 2 * hi, one, 0)

    def arrive(slots):
        for k in slots:
            g.landed("cA%d" % k, "cB%d" % k)

    def base_of(k):
        d, other = pick((0, 0, 1, 3, 1, 3, 2, 2), k), pick((0, 1, 0, 0, 1, 1, 0, 1), k)
        hi, lo = jnp.where(other == 1, 1 - y_hi, y_hi), jnp.where(other == 1, 1 - y_lo, y_lo)
        return (at_txt(lo, x, c) * 8 + ((z + d) % 4) * 2 + hi) * R

    def tile(s, _):
        qp, tp = pick([t[0] for t in TILES], s), pick([t[1] for t in TILES], s)
        rows, cols = rows_at(qp, 4 * R), rows_at(tp, 2 * R)
        dots = lax.dot_general(im[rows, 0:2 * D], tx[cols, :], (((1,), (1,)), ((), ())), preferred_element_type=F32)
        near = rel[rows, :]
        for half in range(2):
            logit = dots[:, half * R:(half + 1) * R] * slope + shift
            positive = near == base_of(2 * tp + half)
            power = jnp.exp2(jnp.where(positive, logit, -logit))
            weight = jnp.where(positive, -upstream, upstream) / (1.0 + power)
            w[rows, rows_at(2 * tp + half, R)] = weight.astype(BF16)
        return 0

    def first():
        g.landed(*both("B3", "B2"))
        g.start(*both("B6t", "B6b", "B5", "B4"), "cB3", "cB2")
        g.landed(*both("A1"))
        g.start(*both("A5", "A4"), "cA1")
        g.landed(*both("B6t", "B6b"))
        g.start(*both("B7"), "cB6")
        g.landed(*both("A3", "A2"))
        g.start(*both("A6"), "cA3", "cA2")
        g.landed(*both("B1"))
        g.start("cB1")
        arrive((0, 1, 2, 3))
        add_up(0, 4)

    def second():
        g.landed(*both("A4"))
        g.start(*both("A7"), "cA4")
        g.landed(*both("A5"))
        g.start("cA5")
        g.landed(*both("B4", "B5"))
        g.start("cB4", "cB5")
        arrive((4, 5))
        add_up(4, 6)

    def third():
        g.landed(*both("A6"))
        g.start("cA6")
        g.landed(*both("A7", "B7"))
        g.start("cA7", "cB7")
        arrive((6, 7))
        add_up(6, 8)

    def part(s, _):
        @pl.when(s == 0)
        def _():
            first()

        @pl.when(s == 4)
        def _():
            second()

        return tile(s, 0)

    lax.fori_loop(0, 9, part, 0)
    third()
    lax.fori_loop(9, len(TILES), tile, 0)
    g.drain()

    r = Copies(r_send, r_recv)
    reduces = (("i", rx_i0, rx_i1, keep_i0, keep_i1, st_i0, st_i1, i_y, i_p, i_m),
               ("t", rx_t0, rx_t1, keep_t0, keep_t1, st_t0, st_t1, t_y, t_p, t_m))
    left, right = ("y0", "y2", "y3", "y6", "pm", "pp", "cc"), ("c1", "f1", "g1", "c2", "f2", "g2", "e1")

    def landing(name, rx0, rx1):
        return rx0.at[left.index(name)] if name in left else rx1.at[right.index(name)]

    for f, rx0, rx1, _, _, s0, s1, y, p, m in reduces:
        def add(name, src, k, to, lo=0, hi=R, into=None, f=f, rx0=rx0, rx1=rx1):
            r.add(f + name, src.at[k, lo:hi], landing(into or name, rx0, rx1).at[lo:hi], to)
        add("c2", s1, 7, m)
        add("y6", s0, 7, y)
        add("c1", s1, 6, p)
        add("g2", s1, 4, p)
        add("y2", s0, 4, y)
        add("g1", s1, 3, m)
        add("y3", s0, 5, y)
        add("y0", s0, 1, y)
        add("ct", s0, 6, p, 0, H, "cc")
        add("cb", s0, 6, m, H, R, "cc")
        add("f2", s1, 5, m)
        add("f1", s1, 2, p)
        add("pmb", s0, 2, p, H, R, "pm")
        add("pmt", s0, 2, p, 0, H, "pm")
        add("ppt", s0, 3, m, 0, H, "pp")
        add("ppb", s0, 3, m, H, R, "pp")
        add("e1", s1, 1, y)

    def core_copy(k):
        return pltpu.make_async_remote_copy(
            src_ref=im.at[rows_at(k, 2 * R), 0:D], dst_ref=rx_core.at[k],
            send_sem=c_send.at[k], recv_sem=c_recv.at[k], device_id=core, device_id_type=MESH)

    def place_of(table, k):
        value = jnp.int32(4)
        for n, entry in enumerate(table):
            value = jnp.where(k == entry, jnp.int32(n), value)
        return value

    def put(k, value, k0, k1, s0, s1):
        value0, value1 = value[:, 0:S], value[:, S:2 * D]
        k0[place_of(KEEP0, k)] = value0
        k1[place_of(KEEP1, k)] = value1
        s0[k] = value0.astype(BF16)
        s1[k] = value1.astype(BF16)

    def send(k, f):
        for slot, names in ((7, ("c2", "y6")), (6, ("c1",)), (4, ("g2", "y2")), (3, ("g1",)), (5, ("y3",)), (1, ("y0",))):
            @pl.when(k == slot)
            def _(names=names):
                r.start(*[f + name for name in names])

    def event(family, do):
        for f, rx0, rx1, k0, k1, s0, s1, *_ in reduces:
            if f == family:
                do(f, lambda name: landing(name, rx0, rx1), k0, k1, s0, s1)

    def after(name, f, rx, k0, k1, s0, s1):
        def got(name, lo=0, hi=R):
            return rx(name)[lo:hi].astype(F32)
        if name == "y6":
            r.landed(f + "y6")
            s0[6] = (k0[KEEP0.index(6)] + got("y6")).astype(BF16)
            r.start(f + "ct", f + "cb")
        elif name == "c2":
            r.landed(f + "c2")
            s1[5] = (k1[KEEP1.index(5)] + got("c2")).astype(BF16)
            r.start(f + "f2")
        elif name == "c1":
            r.landed(f + "c1")
            s1[2] = (k1[KEEP1.index(2)] + got("c1")).astype(BF16)
            r.start(f + "f1")
        elif name == "y2":
            r.landed(f + "y2")
            s0[2, H:R] = (k0[KEEP0.index(2), H:R] + got("y2", H, R)).astype(BF16)
            r.start(f + "pmb")
        elif name == "ct":
            r.landed(f + "ct")
            s0[2, 0:H] = (k0[KEEP0.index(2), 0:H] + got("y2", 0, H) + got("cc", 0, H)).astype(BF16)
            r.start(f + "pmt")
        elif name == "y3":
            r.landed(f + "y3")
            s0[3, 0:H] = (k0[KEEP0.index(3), 0:H] + got("y3", 0, H)).astype(BF16)
            r.start(f + "ppt")
        elif name == "cb":
            r.landed(f + "cb")
            s0[3, H:R] = (k0[KEEP0.index(3), H:R] + got("y3", H, R) + got("cc", H, R)).astype(BF16)
            r.start(f + "ppb")
        elif name == "e1":
            r.landed(f + "g2", f + "f2")
            s1[1] = (k1[KEEP1.index(1)] + got("g2") + got("f2")).astype(BF16)
            r.start(f + "e1")

    def give(k):
        mine, theirs = (pl.ds(pl.multiple_of(k * 2 * R + half, R), R) for half in (0, R))
        part = jnp.dot(w[theirs, :], tx[...], preferred_element_type=F32)
        im[mine, 0:D] = part[:, 0:D].astype(BF16)
        im[theirs, 0:D] = part[:, D:2 * D].astype(BF16)
        core_copy(k).start()

    def follow(n, parity):
        for family, name, at in EVENTS:
            if at < 15 and at % 2 == parity:
                @pl.when(n == at // 2)
                def _(family=family, name=name):
                    event(family, functools.partial(after, name))

    def round_(n, _):
        k = pick(ORDER, n)
        part = lax.dot_general(w[:, rows_at(k, R)], im[:, D:3 * D], (((0,), (0,)), ((), ())), preferred_element_type=F32)
        put(k, part, keep_t0, keep_t1, st_t0, st_t1)
        send(k, "t")
        follow(n, 0)

        @pl.when(n < 7)
        def _():
            give(pick(ORDER, n + 1))

        core_copy(k).wait_recv()
        part = jnp.dot(w[pl.ds(pl.multiple_of(k * 2 * R, R), R), :], tx[...], preferred_element_type=F32)
        part = part + jnp.concatenate([rx_core[k, 0:R], rx_core[k, R:2 * R]], axis=1).astype(F32)
        put(k, part, keep_i0, keep_i1, st_i0, st_i1)
        send(k, "i")
        follow(n, 1)
        return 0

    give(ORDER[0])
    lax.fori_loop(0, 8, round_, 0)
    for family, name, at in EVENTS:
        if at == 15:
            event(family, functools.partial(after, name))

    times = jnp.exp(jnp.broadcast_to(log_temp[...], (1, 2 * D)))
    outs = {"i": (out_img_tan, out_img), "t": (out_txt_tan, out_txt)}

    def finish(f, rx, k0, k1, s0, s1):
        r.landed(f + "y0", f + "pmb", f + "pmt", f + "ppt", f + "ppb")
        low = k0[0] + rx("y0")[...].astype(F32) + rx("pm")[...].astype(F32) + rx("pp")[...].astype(F32)
        r.landed(f + "f1", f + "g1", f + "e1")
        high = k1[0] + rx("f1")[...].astype(F32) + rx("g1")[...].astype(F32) + rx("e1")[...].astype(F32)
        total = times * jnp.concatenate([low, high], axis=1)
        outs[f][0][...] = total[:, 0:D]
        outs[f][1][...] = total[:, D:2 * D]

    event("i", finish)
    event("t", finish)
    r.drain()
    for k in range(8):
        core_copy(k).wait_send()


def copier(a, b, c, d, e, f, g, h, sem):
    copies = [pltpu.make_async_copy(src, dst, sem.at[n])
              for n, (src, dst) in enumerate(((a, e), (b, f), (c, g), (d, h)))]
    for copy in copies:
        copy.start()
    for copy in copies:
        copy.wait()


def body(img_embed, img_tangent, txt_embed, txt_tangent, labels, log_temp, bias, cotangent):
    R, D = txt_embed.shape
    S = split(D)
    vmem = pl.BlockSpec(memory_space=pltpu.VMEM)
    anym = pl.BlockSpec(memory_space=pl.ANY)
    out = pltpu.VMEM((R, D), F32)
    dma = pltpu.SemaphoreType.DMA
    grads = pl.pallas_call(
        kernel,
        out_shape=[out] * 4,
        in_specs=[anym] * 8,
        out_specs=[vmem] * 4,
        scratch_shapes=[
            pltpu.VMEM((16 * R, 3 * D), BF16),
            pltpu.VMEM((8 * R, 2 * D), BF16),
            pltpu.VMEM((R, D), BF16),
            pltpu.VMEM((16 * R, 8 * R), BF16),
            pltpu.VMEM((16 * R, R), jnp.int32),
            pltpu.VMEM((8, 2 * R, D), BF16),
        ] + [pltpu.VMEM((7, R, S), BF16), pltpu.VMEM((7, R, 2 * D - S), BF16)] * 2
        + [pltpu.VMEM((5, R, S), F32), pltpu.VMEM((5, R, 2 * D - S), F32)] * 2
        + [pltpu.VMEM((8, R, S), BF16), pltpu.VMEM((8, R, 2 * D - S), BF16)] * 2
        + [pltpu.VMEM((1, 1), F32)] * 3 + [pltpu.VMEM((16, R), jnp.int32)]
        + [dma((8,)), dma((N_GATHER,)), dma((N_GATHER,)), dma((N_REDUCE,)), dma((N_REDUCE,)), dma((8,)), dma((8,))],
        compiler_params=pltpu.CompilerParams(
            collective_id=0, has_side_effects=True, vmem_limit_bytes=60 * 2 ** 20),
    )(log_temp.reshape(1, 1), bias.reshape(1, 1), cotangent.reshape(1, 1), labels.reshape(16, R), img_embed, img_tangent, txt_embed, txt_tangent)
    grads = pl.pallas_call(
        copier, out_shape=[jax.ShapeDtypeStruct((R, D), F32)] * 4, in_specs=[vmem] * 4, out_specs=[anym] * 4,
        scratch_shapes=[dma((4,))],
    )(*[pltpu.with_memory_space_constraint(grad, pltpu.VMEM) for grad in grads])
    grad_img, grad_img_tangent, grad_txt, grad_txt_tangent = grads
    return grad_img, grad_img_tangent, grad_txt, grad_txt_tangent


def solution(mesh):
    rows = P(("img", "txt"), None)
    cols = P(("txt", "img"), None)
    return jax.shard_map(
        body, mesh=mesh,
        in_specs=(rows, rows, cols, cols, P("img"), P(), P(), P()),
        out_specs=(rows, rows, cols, cols), check_vma=False)
```

```python
import functools
import math

import jax
import jax.numpy as jnp
from jax import lax
from jax.experimental import pallas as pl
from jax.experimental.pallas import tpu as pltpu
from jax.sharding import PartitionSpec as P

MESH = pl.DeviceIdType.MESH
F32 = jnp.float32
BF16 = jnp.bfloat16
LOG2E = math.log2(math.e)

ORDER = (7, 4, 6, 5, 2, 3, 1, 0)
EVENTS = (
    ("t", "y6", 5), ("i", "y6", 7), ("t", "c2", 7), ("i", "c2", 8),
    ("t", "y2", 9), ("i", "y2", 10), ("t", "y3", 13), ("i", "y3", 13),
    ("t", "c1", 13), ("i", "c1", 13), ("t", "cb", 13), ("i", "cb", 13),
    ("t", "e1", 13), ("t", "ct", 14), ("i", "e1", 14), ("i", "ct", 15),
)
KEEP0 = (0, 2, 3, 6)
KEEP1 = (0, 1, 2, 5)
TILES = ((0, 0), (0, 1), (1, 0), (1, 1),
         (0, 2), (1, 2), (2, 0), (2, 1), (2, 2),
         (0, 3), (1, 3), (2, 3))


def pick(table, index):
    value = jnp.int32(table[0])
    for at, entry in enumerate(table[1:], 1):
        value = jnp.where(index == at, jnp.int32(entry), value)
    return value


def rows_at(index, size):
    return pl.ds(pl.multiple_of(index * size, size), size)


def split(D):
    return max(1, round(2 * D * 4 / 9 / 128)) * 128


class Copies:
    def __init__(self, send, recv):
        self.send, self.recv, self.table = send, recv, {}

    def add(self, name, src, dst, device):
        at = len(self.table)
        self.table[name] = pltpu.make_async_remote_copy(
            src_ref=src, dst_ref=dst, send_sem=self.send.at[at], recv_sem=self.recv.at[at],
            device_id=device, device_id_type=MESH)

    def start(self, *names):
        for name in names:
            self.table[name].start()

    def landed(self, *names):
        for name in names:
            self.table[name].wait_recv()

    def drain(self):
        for copy in self.table.values():
            copy.wait_send()


N_GATHER = 15 + 15 + 16
N_REDUCE = 17 + 17


def kernel(log_temp_in, bias_in, cotangent_in, labels_in, img_embed, img_tangent, txt_embed, txt_tangent,
           out_img, out_img_tan, out_txt, out_txt_tan,
           im, tx, tan, w, rel, rx_core, rx_i0, rx_i1, rx_t0, rx_t1, keep_i0, keep_i1, keep_t0, keep_t1,
           st_i0, st_i1, st_t0, st_t1, log_temp, bias, cotangent, labels,
           load_sem, g_send, g_recv, r_send, r_recv, c_send, c_recv):
    R, D = txt_embed.shape
    H = R // 2
    S = split(D)
    img, txt = lax.axis_index("img"), lax.axis_index("txt")
    z, y_hi = img // 2, img % 2
    y_lo, x, c = txt // 8, (txt // 2) % 4, txt % 2

    def at_txt(y_lo, x, c):
        return (y_lo * 4 + x) * 2 + c

    core = (img, at_txt(y_lo, x, 1 - c))
    i_y = (img, at_txt(1 - y_lo, x, c))
    i_p, i_m = (img, at_txt(y_lo, (x + 1) % 4, c)), (img, at_txt(y_lo, (x + 3) % 4, c))
    t_y = (z * 2 + 1 - y_hi, at_txt(1 - y_lo, x, c))
    t_p, t_m = (((z + 1) % 4) * 2 + y_hi, txt), (((z + 3) % 4) * 2 + y_hi, txt)

    loads = [
        pltpu.make_async_copy(src, dst, load_sem.at[n])
        for n, (src, dst) in enumerate((
            (img_embed, im.at[0:R, D:2 * D]), (img_tangent, im.at[0:R, 0:D]),
            (txt_embed, tx.at[0:R, 0:D]), (txt_tangent, tan),
            (log_temp_in, log_temp), (bias_in, bias), (cotangent_in, cotangent), (labels_in, labels)))
    ]
    for copy in loads:
        copy.start()
    barrier = pltpu.get_barrier_semaphore()
    peers = (core, i_y, i_p, i_m, t_y, t_p, t_m)
    for peer in peers:
        pl.semaphore_signal(barrier, inc=1, device_id=peer, device_id_type=MESH)
    for copy in loads:
        copy.wait()
    tx[0:R, D:2 * D] = (tx[0:R, 0:D].astype(F32) + tan[...].astype(F32)).astype(BF16)
    pl.semaphore_wait(barrier, len(peers))

    g = Copies(g_send, g_recv)
    families = (("i", im, 2 * R, i_y, i_p, i_m), ("t", tx, R, t_y, t_p, t_m))
    a, b = slice(S, 2 * D), slice(0, S)
    for f, buf, pitch, y, p, m in families:
        def add(name, src, dst, col, to, lo=0, hi=R, f=f, buf=buf, pitch=pitch):
            g.add(f + name, buf.at[src * pitch + lo:src * pitch + hi, col],
                  buf.at[dst * pitch + lo:dst * pitch + hi, col], to)
        add("A1", 0, 1, a, y)
        add("A3", 0, 3, a, p)
        add("A2", 0, 2, a, m)
        add("A5", 1, 5, a, p)
        add("A4", 1, 4, a, m)
        add("A6", 3, 6, a, p)
        add("A7", 4, 7, a, m)
        add("B3", 0, 3, b, p)
        add("B2", 0, 2, b, m)
        add("B6t", 3, 6, b, p, 0, H)
        add("B6b", 2, 6, b, m, H, R)
        add("B1", 0, 1, b, y)
        add("B4", 2, 4, b, y)
        add("B5", 3, 5, b, y)
        add("B7", 6, 7, b, y)
    for k in range(8):
        for name, col in (("A", a), ("B", b)):
            g.add("c%s%d" % (name, k), im.at[2 * R * k:2 * R * k + R, col],
                  im.at[2 * R * k + R:2 * R * (k + 1), col], core)

    def both(*names):
        return [f + name for name in names for f in "it"]

    g.start(*both("A1", "B3", "B2", "A3", "A2", "B1"), "cB0", "cA0")

    lane = lax.broadcasted_iota(jnp.int32, (R, R), 1)

    def place(k, _):
        shift, other = pick((0, 0, 1, 3, 1, 3, 2, 2), k // 2), pick((0, 1, 0, 0, 1, 1, 0, 1), k // 2)
        t = at_txt(jnp.where(other == 1, 1 - y_lo, y_lo), (x + shift) % 4, jnp.where(k % 2 == 1, 1 - c, c))
        row = jnp.broadcast_to(labels[pl.ds(t, 1), :], (R, R))
        rel[rows_at(k, R), :] = row.T - lane
        return 0

    lax.fori_loop(0, 16, place, 0)

    scale = jnp.exp(jnp.broadcast_to(log_temp[...], (1, R)))
    slope, shift = scale * LOG2E, jnp.broadcast_to(bias[...], (1, R)) * LOG2E
    upstream = jnp.broadcast_to(cotangent[...], (1, R))

    def add_up(lo, hi):
        def one(k, _):
            rows = rows_at(k, R)
            im[rows, 2 * D:3 * D] = (im[rows, 0:D].astype(F32) + im[rows, D:2 * D].astype(F32)).astype(BF16)
            return 0
        lax.fori_loop(2 * lo, 2 * hi, one, 0)

    def arrive(slots):
        for k in slots:
            g.landed("cA%d" % k, "cB%d" % k)

    def base_of(k):
        d, other = pick((0, 0, 1, 3, 1, 3, 2, 2), k), pick((0, 1, 0, 0, 1, 1, 0, 1), k)
        hi, lo = jnp.where(other == 1, 1 - y_hi, y_hi), jnp.where(other == 1, 1 - y_lo, y_lo)
        return (at_txt(lo, x, c) * 8 + ((z + d) % 4) * 2 + hi) * R

    def weigh(dots, rows, first, count):
        near = rel[rows, :]
        for n in range(count):
            logit = dots[:, n * R:(n + 1) * R] * slope + shift
            positive = near == base_of(first + n)
            power = jnp.exp2(jnp.where(positive, logit, -logit))
            weight = jnp.where(positive, -upstream, upstream) / (1.0 + power)
            w[rows, rows_at(first + n, R)] = weight.astype(BF16)

    def tile(s, _):
        qp, tp = pick([t[0] for t in TILES], s), pick([t[1] for t in TILES], s)
        rows, cols = rows_at(qp, 4 * R), rows_at(tp, 2 * R)
        dots = lax.dot_general(im[rows, 0:2 * D], tx[cols, :], (((1,), (1,)), ((), ())), preferred_element_type=F32)
        weigh(dots, rows, 2 * tp, 2)
        return 0

    def first():
        g.landed(*both("B3", "B2"))
        g.start(*both("B6t", "B6b", "B5", "B4"), "cB3", "cB2")
        g.landed(*both("A1"))
        g.start(*both("A5", "A4"), "cA1")
        g.landed(*both("B6t", "B6b"))
        g.start(*both("B7"), "cB6")
        g.landed(*both("A3", "A2"))
        g.start(*both("A6"), "cA3", "cA2")
        g.landed(*both("B1"))
        g.start("cB1")
        arrive((0, 1, 2, 3))
        add_up(0, 4)

    def forward():
        g.landed(*both("A4"))
        g.start(*both("A7"), "cA4")

    def second():
        for name in ("B5", "A5", "B4"):
            g.landed("i" + name)
            g.start("c" + name)
        g.landed("tB5", "tA5", "tB4")

    def second_img():
        arrive((4, 5))

    def third():
        add_up(4, 6)
        for name in ("A6", "A7", "B7"):
            g.landed("i" + name)
            g.start("c" + name)
        g.landed("tA6", "tA7", "tB7")

    def third_img():
        arrive((6, 7))

    def part(s, _):
        for at, do in ((0, first), (2, forward), (4, second), (6, second_img), (9, third)):
            @pl.when(s == at)
            def _(do=do):
                do()

        return tile(s, 0)

    lax.fori_loop(0, 12, part, 0)
    third_img()
    rows = pl.ds(12 * R, 4 * R)
    weigh(lax.dot_general(im[rows, 0:2 * D], tx[...], (((1,), (1,)), ((), ())), preferred_element_type=F32), rows, 0, 8)
    add_up(6, 8)
    g.drain()

    r = Copies(r_send, r_recv)
    reduces = (("i", rx_i0, rx_i1, keep_i0, keep_i1, st_i0, st_i1, i_y, i_p, i_m),
               ("t", rx_t0, rx_t1, keep_t0, keep_t1, st_t0, st_t1, t_y, t_p, t_m))
    left, right = ("y0", "y2", "y3", "y6", "pm", "pp", "cc"), ("c1", "f1", "g1", "c2", "f2", "g2", "e1")

    def landing(name, rx0, rx1):
        return rx0.at[left.index(name)] if name in left else rx1.at[right.index(name)]

    for f, rx0, rx1, _, _, s0, s1, y, p, m in reduces:
        def add(name, src, k, to, lo=0, hi=R, into=None, f=f, rx0=rx0, rx1=rx1):
            r.add(f + name, src.at[k, lo:hi], landing(into or name, rx0, rx1).at[lo:hi], to)
        add("c2", s1, 7, m)
        add("y6", s0, 7, y)
        add("c1", s1, 6, p)
        add("g2", s1, 4, p)
        add("y2", s0, 4, y)
        add("g1", s1, 3, m)
        add("y3", s0, 5, y)
        add("y0", s0, 1, y)
        add("ct", s0, 6, p, 0, H, "cc")
        add("cb", s0, 6, m, H, R, "cc")
        add("f2", s1, 5, m)
        add("f1", s1, 2, p)
        add("pmb", s0, 2, p, H, R, "pm")
        add("pmt", s0, 2, p, 0, H, "pm")
        add("ppt", s0, 3, m, 0, H, "pp")
        add("ppb", s0, 3, m, H, R, "pp")
        add("e1", s1, 1, y)

    def core_copy(k):
        return pltpu.make_async_remote_copy(
            src_ref=im.at[rows_at(k, 2 * R), 0:D], dst_ref=rx_core.at[k],
            send_sem=c_send.at[k], recv_sem=c_recv.at[k], device_id=core, device_id_type=MESH)

    def place_of(table, k):
        value = jnp.int32(4)
        for n, entry in enumerate(table):
            value = jnp.where(k == entry, jnp.int32(n), value)
        return value

    def put(k, value, k0, k1, s0, s1):
        value0, value1 = value[:, 0:S], value[:, S:2 * D]
        k0[place_of(KEEP0, k)] = value0
        k1[place_of(KEEP1, k)] = value1
        s0[k] = value0.astype(BF16)
        s1[k] = value1.astype(BF16)

    def send(k, f):
        for slot, names in ((7, ("c2", "y6")), (6, ("c1",)), (4, ("g2", "y2")), (3, ("g1",)), (5, ("y3",)), (1, ("y0",))):
            @pl.when(k == slot)
            def _(names=names):
                r.start(*[f + name for name in names])

    def event(family, do):
        for f, rx0, rx1, k0, k1, s0, s1, *_ in reduces:
            if f == family:
                do(f, lambda name: landing(name, rx0, rx1), k0, k1, s0, s1)

    def after(name, f, rx, k0, k1, s0, s1):
        def got(name, lo=0, hi=R):
            return rx(name)[lo:hi].astype(F32)
        if name == "y6":
            r.landed(f + "y6")
            s0[6] = (k0[KEEP0.index(6)] + got("y6")).astype(BF16)
            r.start(f + "ct", f + "cb")
        elif name == "c2":
            r.landed(f + "c2")
            s1[5] = (k1[KEEP1.index(5)] + got("c2")).astype(BF16)
            r.start(f + "f2")
        elif name == "c1":
            r.landed(f + "c1")
            s1[2] = (k1[KEEP1.index(2)] + got("c1")).astype(BF16)
            r.start(f + "f1")
        elif name == "y2":
            r.landed(f + "y2")
            s0[2, H:R] = (k0[KEEP0.index(2), H:R] + got("y2", H, R)).astype(BF16)
            r.start(f + "pmb")
        elif name == "ct":
            r.landed(f + "ct")
            s0[2, 0:H] = (k0[KEEP0.index(2), 0:H] + got("y2", 0, H) + got("cc", 0, H)).astype(BF16)
            r.start(f + "pmt")
        elif name == "y3":
            r.landed(f + "y3")
            s0[3, 0:H] = (k0[KEEP0.index(3), 0:H] + got("y3", 0, H)).astype(BF16)
            r.start(f + "ppt")
        elif name == "cb":
            r.landed(f + "cb")
            s0[3, H:R] = (k0[KEEP0.index(3), H:R] + got("y3", H, R) + got("cc", H, R)).astype(BF16)
            r.start(f + "ppb")
        elif name == "e1":
            r.landed(f + "g2", f + "f2")
            s1[1] = (k1[KEEP1.index(1)] + got("g2") + got("f2")).astype(BF16)
            r.start(f + "e1")

    def give(k):
        mine, theirs = (pl.ds(pl.multiple_of(k * 2 * R + half, R), R) for half in (0, R))
        part = jnp.dot(w[theirs, :], tx[...], preferred_element_type=F32)
        im[mine, 0:D] = part[:, 0:D].astype(BF16)
        im[theirs, 0:D] = part[:, D:2 * D].astype(BF16)
        core_copy(k).start()

    def follow(n, parity):
        for family, name, at in EVENTS:
            if at < 15 and at % 2 == parity:
                @pl.when(n == at // 2)
                def _(family=family, name=name):
                    event(family, functools.partial(after, name))

    def round_(n, _):
        k = pick(ORDER, n)
        part = lax.dot_general(w[:, rows_at(k, R)], im[:, D:3 * D], (((0,), (0,)), ((), ())), preferred_element_type=F32)
        put(k, part, keep_t0, keep_t1, st_t0, st_t1)
        send(k, "t")
        follow(n, 0)

        @pl.when(n < 7)
        def _():
            give(pick(ORDER, n + 1))

        core_copy(k).wait_recv()
        part = jnp.dot(w[pl.ds(pl.multiple_of(k * 2 * R, R), R), :], tx[...], preferred_element_type=F32)
        part = part + jnp.concatenate([rx_core[k, 0:R], rx_core[k, R:2 * R]], axis=1).astype(F32)
        put(k, part, keep_i0, keep_i1, st_i0, st_i1)
        send(k, "i")
        follow(n, 1)
        return 0

    give(ORDER[0])
    lax.fori_loop(0, 8, round_, 0)
    for family, name, at in EVENTS:
        if at == 15:
            event(family, functools.partial(after, name))

    times = jnp.exp(jnp.broadcast_to(log_temp[...], (1, S)))
    outs = {"i": (out_img_tan, out_img), "t": (out_txt_tan, out_txt)}

    def finish_left(f, rx, k0, k1, s0, s1):
        r.landed(f + "y0", f + "pmb", f + "pmt", f + "ppt", f + "ppb")
        total = k0[0] + rx("y0")[...].astype(F32) + rx("pm")[...].astype(F32) + rx("pp")[...].astype(F32)
        outs[f][0][:, 0:S] = times * total

    def finish_right(f, rx, k0, k1, s0, s1):
        r.landed(f + "f1", f + "g1", f + "e1")
        total = k1[0] + rx("f1")[...].astype(F32) + rx("g1")[...].astype(F32) + rx("e1")[...].astype(F32)
        total = jnp.broadcast_to(times[:, 0:1], total.shape) * total
        outs[f][0][:, S:D] = total[:, 0:D - S]
        outs[f][1][...] = total[:, D - S:]

    event("t", finish_left)
    event("i", finish_left)
    event("t", finish_right)
    event("i", finish_right)
    r.drain()
    for k in range(8):
        core_copy(k).wait_send()


def copier(a, b, c, d, e, f, g, h, sem):
    copies = [pltpu.make_async_copy(src, dst, sem.at[n])
              for n, (src, dst) in enumerate(((a, e), (b, f), (c, g), (d, h)))]
    for copy in copies:
        copy.start()
    for copy in copies:
        copy.wait()


def body(img_embed, img_tangent, txt_embed, txt_tangent, labels, log_temp, bias, cotangent):
    R, D = txt_embed.shape
    S = split(D)
    vmem = pl.BlockSpec(memory_space=pltpu.VMEM)
    anym = pl.BlockSpec(memory_space=pl.ANY)
    out = pltpu.VMEM((R, D), F32)
    dma = pltpu.SemaphoreType.DMA
    grads = pl.pallas_call(
        kernel,
        out_shape=[out] * 4,
        in_specs=[anym] * 8,
        out_specs=[vmem] * 4,
        scratch_shapes=[
            pltpu.VMEM((16 * R, 3 * D), BF16),
            pltpu.VMEM((8 * R, 2 * D), BF16),
            pltpu.VMEM((R, D), BF16),
            pltpu.VMEM((16 * R, 8 * R), BF16),
            pltpu.VMEM((16 * R, R), jnp.int32),
            pltpu.VMEM((8, 2 * R, D), BF16),
        ] + [pltpu.VMEM((7, R, S), BF16), pltpu.VMEM((7, R, 2 * D - S), BF16)] * 2
        + [pltpu.VMEM((5, R, S), F32), pltpu.VMEM((5, R, 2 * D - S), F32)] * 2
        + [pltpu.VMEM((8, R, S), BF16), pltpu.VMEM((8, R, 2 * D - S), BF16)] * 2
        + [pltpu.VMEM((1, 1), F32)] * 3 + [pltpu.VMEM((16, R), jnp.int32)]
        + [dma((8,)), dma((N_GATHER,)), dma((N_GATHER,)), dma((N_REDUCE,)), dma((N_REDUCE,)), dma((8,)), dma((8,))],
        compiler_params=pltpu.CompilerParams(
            collective_id=0, has_side_effects=True, vmem_limit_bytes=60 * 2 ** 20),
    )(log_temp.reshape(1, 1), bias.reshape(1, 1), cotangent.reshape(1, 1), labels.reshape(16, R), img_embed, img_tangent, txt_embed, txt_tangent)
    grads = pl.pallas_call(
        copier, out_shape=[jax.ShapeDtypeStruct((R, D), F32)] * 4, in_specs=[vmem] * 4, out_specs=[anym] * 4,
        scratch_shapes=[dma((4,))],
    )(*[pltpu.with_memory_space_constraint(grad, pltpu.VMEM) for grad in grads])
    grad_img, grad_img_tangent, grad_txt, grad_txt_tangent = grads
    return grad_img, grad_img_tangent, grad_txt, grad_txt_tangent


def solution(mesh):
    rows = P(("img", "txt"), None)
    cols = P(("txt", "img"), None)
    return jax.shard_map(
        body, mesh=mesh,
        in_specs=(rows, rows, cols, cols, P("img"), P(), P(), P()),
        out_specs=(rows, rows, cols, cols), check_vma=False)
```

```python
import functools
import math

import jax
import jax.numpy as jnp
from jax import lax
from jax.experimental import pallas as pl
from jax.experimental.pallas import tpu as pltpu
from jax.sharding import PartitionSpec as P

MESH = pl.DeviceIdType.MESH
F32 = jnp.float32
BF16 = jnp.bfloat16
LOG2E = math.log2(math.e)

ORDER = (7, 4, 6, 5, 2, 3, 1, 0)
EVENTS = (
    ("t", "y6", 5), ("i", "y6", 7), ("t", "c2", 7), ("i", "c2", 8),
    ("t", "y2", 9), ("i", "y2", 10), ("t", "y3", 13), ("i", "y3", 13),
    ("t", "c1", 13), ("i", "c1", 13), ("t", "cb", 13), ("i", "cb", 13),
    ("t", "e1", 13), ("t", "ct", 14), ("i", "e1", 14), ("i", "ct", 15),
)
KEEP0 = (0, 2, 3, 6)
KEEP1 = (0, 1, 2, 5)
TILES = ((0, 0), (0, 1), (1, 0), (1, 1),
         (0, 2), (1, 2), (2, 0), (2, 1), (2, 2),
         (0, 3), (1, 3), (2, 3))


def pick(table, index):
    value = jnp.int32(table[0])
    for at, entry in enumerate(table[1:], 1):
        value = jnp.where(index == at, jnp.int32(entry), value)
    return value


def rows_at(index, size):
    return pl.ds(pl.multiple_of(index * size, size), size)


def split(D):
    return max(1, round(2 * D * 4 / 9 / 128)) * 128


class Copies:
    def __init__(self, send, recv):
        self.send, self.recv, self.table = send, recv, {}

    def add(self, name, src, dst, device):
        at = len(self.table)
        self.table[name] = pltpu.make_async_remote_copy(
            src_ref=src, dst_ref=dst, send_sem=self.send.at[at], recv_sem=self.recv.at[at],
            device_id=device, device_id_type=MESH)

    def start(self, *names):
        for name in names:
            self.table[name].start()

    def landed(self, *names):
        for name in names:
            self.table[name].wait_recv()

    def drain(self):
        for copy in self.table.values():
            copy.wait_send()


N_GATHER = 15 + 15 + 16
N_REDUCE = 17 + 17


def kernel(log_temp_in, bias_in, cotangent_in, labels_in, img_embed, img_tangent, txt_embed, txt_tangent,
           out_img, out_img_tan, out_txt, out_txt_tan,
           im, tx, tan, w, rel, rx_core, rx_i0, rx_i1, rx_t0, rx_t1, keep_i0, keep_i1, keep_t0, keep_t1,
           st_i0, st_i1, st_t0, st_t1, log_temp, bias, cotangent, labels,
           load_sem, g_send, g_recv, r_send, r_recv, c_send, c_recv):
    R, D = txt_embed.shape
    H = R // 2
    S = split(D)
    img, txt = lax.axis_index("img"), lax.axis_index("txt")
    z, y_hi = img // 2, img % 2
    y_lo, x, c = txt // 8, (txt // 2) % 4, txt % 2

    def at_txt(y_lo, x, c):
        return (y_lo * 4 + x) * 2 + c

    core = (img, at_txt(y_lo, x, 1 - c))
    i_y = (img, at_txt(1 - y_lo, x, c))
    i_p, i_m = (img, at_txt(y_lo, (x + 1) % 4, c)), (img, at_txt(y_lo, (x + 3) % 4, c))
    t_y = (z * 2 + 1 - y_hi, at_txt(1 - y_lo, x, c))
    t_p, t_m = (((z + 1) % 4) * 2 + y_hi, txt), (((z + 3) % 4) * 2 + y_hi, txt)

    loads = [
        pltpu.make_async_copy(src, dst, load_sem.at[n])
        for n, (src, dst) in enumerate((
            (img_embed, im.at[0:R, D:2 * D]), (img_tangent, im.at[0:R, 0:D]),
            (txt_embed, tx.at[0:R, 0:D]), (txt_tangent, tan),
            (log_temp_in, log_temp), (bias_in, bias), (cotangent_in, cotangent), (labels_in, labels)))
    ]
    for copy in loads:
        copy.start()
    barrier = pltpu.get_barrier_semaphore()
    peers = (core, i_y, i_p, i_m, t_y, t_p, t_m)
    for peer in peers:
        pl.semaphore_signal(barrier, inc=1, device_id=peer, device_id_type=MESH)
    for copy in loads[0:2]:
        copy.wait()
    pl.semaphore_wait(barrier, len(peers))

    g = Copies(g_send, g_recv)
    families = (("i", im, 2 * R, i_y, i_p, i_m), ("t", tx, R, t_y, t_p, t_m))
    a, b = slice(S, 2 * D), slice(0, S)
    for f, buf, pitch, y, p, m in families:
        def add(name, src, dst, col, to, lo=0, hi=R, f=f, buf=buf, pitch=pitch):
            g.add(f + name, buf.at[src * pitch + lo:src * pitch + hi, col],
                  buf.at[dst * pitch + lo:dst * pitch + hi, col], to)
        add("A1", 0, 1, a, y)
        add("A3", 0, 3, a, p)
        add("A2", 0, 2, a, m)
        add("A5", 1, 5, a, p)
        add("A4", 1, 4, a, m)
        add("A6", 3, 6, a, p)
        add("A7", 4, 7, a, m)
        add("B3", 0, 3, b, p)
        add("B2", 0, 2, b, m)
        add("B6t", 3, 6, b, p, 0, H)
        add("B6b", 2, 6, b, m, H, R)
        add("B1", 0, 1, b, y)
        add("B4", 2, 4, b, y)
        add("B5", 3, 5, b, y)
        add("B7", 6, 7, b, y)
    for k in range(8):
        for name, col in (("A", a), ("B", b)):
            g.add("c%s%d" % (name, k), im.at[2 * R * k:2 * R * k + R, col],
                  im.at[2 * R * k + R:2 * R * (k + 1), col], core)

    def both(*names):
        return [f + name for name in names for f in "it"]

    g.start("iA1", "iB3", "iB2", "iA3", "iA2", "iB1")
    for copy in loads[2:4]:
        copy.wait()
    tx[0:R, D:2 * D] = (tx[0:R, 0:D].astype(F32) + tan[...].astype(F32)).astype(BF16)
    g.start("tA1", "tB3", "tB2", "tA3", "tA2", "tB1", "cB0", "cA0")
    for copy in loads[4:]:
        copy.wait()

    lane = lax.broadcasted_iota(jnp.int32, (R, R), 1)

    def place(k, _):
        shift, other = pick((0, 0, 1, 3, 1, 3, 2, 2), k // 2), pick((0, 1, 0, 0, 1, 1, 0, 1), k // 2)
        t = at_txt(jnp.where(other == 1, 1 - y_lo, y_lo), (x + shift) % 4, jnp.where(k % 2 == 1, 1 - c, c))
        row = jnp.broadcast_to(labels[pl.ds(t, 1), :], (R, R))
        rel[rows_at(k, R), :] = row.T - lane
        return 0

    lax.fori_loop(0, 16, place, 0)

    scale = jnp.exp(jnp.broadcast_to(log_temp[...], (1, R)))
    slope, shift = scale * LOG2E, jnp.broadcast_to(bias[...], (1, R)) * LOG2E
    upstream = jnp.broadcast_to(cotangent[...], (1, R))

    def add_up(lo, hi):
        def one(k, _):
            rows = rows_at(k, R)
            im[rows, 2 * D:3 * D] = (im[rows, 0:D].astype(F32) + im[rows, D:2 * D].astype(F32)).astype(BF16)
            return 0
        lax.fori_loop(2 * lo, 2 * hi, one, 0)

    def arrive(slots):
        for k in slots:
            g.landed("cA%d" % k, "cB%d" % k)

    def base_of(k):
        d, other = pick((0, 0, 1, 3, 1, 3, 2, 2), k), pick((0, 1, 0, 0, 1, 1, 0, 1), k)
        hi, lo = jnp.where(other == 1, 1 - y_hi, y_hi), jnp.where(other == 1, 1 - y_lo, y_lo)
        return (at_txt(lo, x, c) * 8 + ((z + d) % 4) * 2 + hi) * R

    def weigh(dots, rows, first, count):
        near = rel[rows, :]
        for n in range(count):
            logit = dots[:, n * R:(n + 1) * R] * slope + shift
            positive = near == base_of(first + n)
            power = jnp.exp2(jnp.where(positive, logit, -logit))
            weight = jnp.where(positive, -upstream, upstream) / (1.0 + power)
            w[rows, rows_at(first + n, R)] = weight.astype(BF16)

    def tile(s, _):
        qp, tp = pick([t[0] for t in TILES], s), pick([t[1] for t in TILES], s)
        rows, cols = rows_at(qp, 4 * R), rows_at(tp, 2 * R)
        dots = lax.dot_general(im[rows, 0:2 * D], tx[cols, :], (((1,), (1,)), ((), ())), preferred_element_type=F32)
        weigh(dots, rows, 2 * tp, 2)
        return 0

    def first():
        g.landed(*both("B3", "B2"))
        g.start(*both("B6t", "B6b", "B5", "B4"), "cB3", "cB2")
        g.landed(*both("A1"))
        g.start(*both("A5", "A4"), "cA1")
        g.landed(*both("B6t", "B6b"))
        g.start(*both("B7"), "cB6")
        g.landed(*both("A3", "A2"))
        g.start(*both("A6"), "cA3", "cA2")
        g.landed(*both("B1"))
        g.start("cB1")
        arrive((0, 1, 2, 3))
        add_up(0, 4)

    def forward():
        g.landed(*both("A4"))
        g.start(*both("A7"), "cA4")

    def second():
        for name in ("B5", "A5", "B4"):
            g.landed("i" + name)
            g.start("c" + name)
        g.landed("tB5", "tA5", "tB4")

    def second_img():
        arrive((4, 5))

    def third():
        add_up(4, 6)
        for name in ("A6", "A7", "B7"):
            g.landed("i" + name)
            g.start("c" + name)
        g.landed("tA6", "tA7", "tB7")

    def third_img():
        arrive((6, 7))

    def part(s, _):
        for at, do in ((0, first), (2, forward), (4, second), (6, second_img), (9, third)):
            @pl.when(s == at)
            def _(do=do):
                do()

        return tile(s, 0)

    lax.fori_loop(0, 12, part, 0)
    third_img()
    rows = pl.ds(12 * R, 4 * R)
    weigh(lax.dot_general(im[rows, 0:2 * D], tx[...], (((1,), (1,)), ((), ())), preferred_element_type=F32), rows, 0, 8)
    add_up(6, 8)
    g.drain()

    r = Copies(r_send, r_recv)
    reduces = (("i", rx_i0, rx_i1, keep_i0, keep_i1, st_i0, st_i1, i_y, i_p, i_m),
               ("t", rx_t0, rx_t1, keep_t0, keep_t1, st_t0, st_t1, t_y, t_p, t_m))
    left, right = ("y0", "y2", "y3", "y6", "pm", "pp", "cc"), ("c1", "f1", "g1", "c2", "f2", "g2", "e1")

    def landing(name, rx0, rx1):
        return rx0.at[left.index(name)] if name in left else rx1.at[right.index(name)]

    for f, rx0, rx1, _, _, s0, s1, y, p, m in reduces:
        def add(name, src, k, to, lo=0, hi=R, into=None, f=f, rx0=rx0, rx1=rx1):
            r.add(f + name, src.at[k, lo:hi], landing(into or name, rx0, rx1).at[lo:hi], to)
        add("c2", s1, 7, m)
        add("y6", s0, 7, y)
        add("c1", s1, 6, p)
        add("g2", s1, 4, p)
        add("y2", s0, 4, y)
        add("g1", s1, 3, m)
        add("y3", s0, 5, y)
        add("y0", s0, 1, y)
        add("ct", s0, 6, p, 0, H, "cc")
        add("cb", s0, 6, m, H, R, "cc")
        add("f2", s1, 5, m)
        add("f1", s1, 2, p)
        add("pmb", s0, 2, p, H, R, "pm")
        add("pmt", s0, 2, p, 0, H, "pm")
        add("ppt", s0, 3, m, 0, H, "pp")
        add("ppb", s0, 3, m, H, R, "pp")
        add("e1", s1, 1, y)

    def core_copy(k):
        return pltpu.make_async_remote_copy(
            src_ref=im.at[rows_at(k, 2 * R), 0:D], dst_ref=rx_core.at[k],
            send_sem=c_send.at[k], recv_sem=c_recv.at[k], device_id=core, device_id_type=MESH)

    def place_of(table, k):
        value = jnp.int32(4)
        for n, entry in enumerate(table):
            value = jnp.where(k == entry, jnp.int32(n), value)
        return value

    def put(k, value, k0, k1, s0, s1):
        value0, value1 = value[:, 0:S], value[:, S:2 * D]
        k0[place_of(KEEP0, k)] = value0
        k1[place_of(KEEP1, k)] = value1
        s0[k] = value0.astype(BF16)
        s1[k] = value1.astype(BF16)

    def send(k, f):
        for slot, names in ((7, ("c2", "y6")), (6, ("c1",)), (4, ("g2", "y2")), (3, ("g1",)), (5, ("y3",)), (1, ("y0",))):
            @pl.when(k == slot)
            def _(names=names):
                r.start(*[f + name for name in names])

    def event(family, do):
        for f, rx0, rx1, k0, k1, s0, s1, *_ in reduces:
            if f == family:
                do(f, lambda name: landing(name, rx0, rx1), k0, k1, s0, s1)

    def after(name, f, rx, k0, k1, s0, s1):
        def got(name, lo=0, hi=R):
            return rx(name)[lo:hi].astype(F32)
        if name == "y6":
            r.landed(f + "y6")
            s0[6] = (k0[KEEP0.index(6)] + got("y6")).astype(BF16)
            r.start(f + "ct", f + "cb")
        elif name == "c2":
            r.landed(f + "c2")
            s1[5] = (k1[KEEP1.index(5)] + got("c2")).astype(BF16)
            r.start(f + "f2")
        elif name == "c1":
            r.landed(f + "c1")
            s1[2] = (k1[KEEP1.index(2)] + got("c1")).astype(BF16)
            r.start(f + "f1")
        elif name == "y2":
            r.landed(f + "y2")
            s0[2, H:R] = (k0[KEEP0.index(2), H:R] + got("y2", H, R)).astype(BF16)
            r.start(f + "pmb")
        elif name == "ct":
            r.landed(f + "ct")
            s0[2, 0:H] = (k0[KEEP0.index(2), 0:H] + got("y2", 0, H) + got("cc", 0, H)).astype(BF16)
            r.start(f + "pmt")
        elif name == "y3":
            r.landed(f + "y3")
            s0[3, 0:H] = (k0[KEEP0.index(3), 0:H] + got("y3", 0, H)).astype(BF16)
            r.start(f + "ppt")
        elif name == "cb":
            r.landed(f + "cb")
            s0[3, H:R] = (k0[KEEP0.index(3), H:R] + got("y3", H, R) + got("cc", H, R)).astype(BF16)
            r.start(f + "ppb")
        elif name == "e1":
            r.landed(f + "g2", f + "f2")
            s1[1] = (k1[KEEP1.index(1)] + got("g2") + got("f2")).astype(BF16)
            r.start(f + "e1")

    def give(k):
        mine, theirs = (pl.ds(pl.multiple_of(k * 2 * R + half, R), R) for half in (0, R))
        part = jnp.dot(w[theirs, :], tx[...], preferred_element_type=F32)
        im[mine, 0:D] = part[:, 0:D].astype(BF16)
        im[theirs, 0:D] = part[:, D:2 * D].astype(BF16)
        core_copy(k).start()

    def follow(n, parity):
        for family, name, at in EVENTS:
            if at < 15 and at % 2 == parity:
                @pl.when(n == at // 2)
                def _(family=family, name=name):
                    event(family, functools.partial(after, name))

    def round_(n, _):
        k = pick(ORDER, n)
        part = lax.dot_general(w[:, rows_at(k, R)], im[:, D:3 * D], (((0,), (0,)), ((), ())), preferred_element_type=F32)
        put(k, part, keep_t0, keep_t1, st_t0, st_t1)
        send(k, "t")
        follow(n, 0)

        @pl.when(n < 7)
        def _():
            give(pick(ORDER, n + 1))

        core_copy(k).wait_recv()
        part = jnp.dot(w[pl.ds(pl.multiple_of(k * 2 * R, R), R), :], tx[...], preferred_element_type=F32)
        part = part + jnp.concatenate([rx_core[k, 0:R], rx_core[k, R:2 * R]], axis=1).astype(F32)
        put(k, part, keep_i0, keep_i1, st_i0, st_i1)
        send(k, "i")
        follow(n, 1)
        return 0

    give(ORDER[0])
    lax.fori_loop(0, 8, round_, 0)
    for family, name, at in EVENTS:
        if at == 15:
            event(family, functools.partial(after, name))

    times = jnp.exp(jnp.broadcast_to(log_temp[...], (1, S)))
    outs = {"i": (out_img_tan, out_img), "t": (out_txt_tan, out_txt)}

    def finish_left(f, rx, k0, k1, s0, s1):
        r.landed(f + "y0", f + "pmb", f + "pmt", f + "ppt", f + "ppb")
        total = k0[0] + rx("y0")[...].astype(F32) + rx("pm")[...].astype(F32) + rx("pp")[...].astype(F32)
        outs[f][0][:, 0:S] = times * total

    def finish_right(f, rx, k0, k1, s0, s1):
        r.landed(f + "f1", f + "g1", f + "e1")
        total = k1[0] + rx("f1")[...].astype(F32) + rx("g1")[...].astype(F32) + rx("e1")[...].astype(F32)
        total = jnp.broadcast_to(times[:, 0:1], total.shape) * total
        outs[f][0][:, S:D] = total[:, 0:D - S]
        outs[f][1][...] = total[:, D - S:]

    event("t", finish_left)
    event("i", finish_left)
    event("t", finish_right)
    event("i", finish_right)
    r.drain()
    for k in range(8):
        core_copy(k).wait_send()


def copier(a, b, c, d, e, f, g, h, sem):
    copies = [pltpu.make_async_copy(src, dst, sem.at[n])
              for n, (src, dst) in enumerate(((a, e), (b, f), (c, g), (d, h)))]
    for copy in copies:
        copy.start()
    for copy in copies:
        copy.wait()


def body(img_embed, img_tangent, txt_embed, txt_tangent, labels, log_temp, bias, cotangent):
    R, D = txt_embed.shape
    S = split(D)
    vmem = pl.BlockSpec(memory_space=pltpu.VMEM)
    anym = pl.BlockSpec(memory_space=pl.ANY)
    out = pltpu.VMEM((R, D), F32)
    dma = pltpu.SemaphoreType.DMA
    grads = pl.pallas_call(
        kernel,
        out_shape=[out] * 4,
        in_specs=[anym] * 8,
        out_specs=[vmem] * 4,
        scratch_shapes=[
            pltpu.VMEM((16 * R, 3 * D), BF16),
            pltpu.VMEM((8 * R, 2 * D), BF16),
            pltpu.VMEM((R, D), BF16),
            pltpu.VMEM((16 * R, 8 * R), BF16),
            pltpu.VMEM((16 * R, R), jnp.int32),
            pltpu.VMEM((8, 2 * R, D), BF16),
        ] + [pltpu.VMEM((7, R, S), BF16), pltpu.VMEM((7, R, 2 * D - S), BF16)] * 2
        + [pltpu.VMEM((5, R, S), F32), pltpu.VMEM((5, R, 2 * D - S), F32)] * 2
        + [pltpu.VMEM((8, R, S), BF16), pltpu.VMEM((8, R, 2 * D - S), BF16)] * 2
        + [pltpu.VMEM((1, 1), F32)] * 3 + [pltpu.VMEM((16, R), jnp.int32)]
        + [dma((8,)), dma((N_GATHER,)), dma((N_GATHER,)), dma((N_REDUCE,)), dma((N_REDUCE,)), dma((8,)), dma((8,))],
        compiler_params=pltpu.CompilerParams(
            collective_id=0, has_side_effects=True, vmem_limit_bytes=60 * 2 ** 20),
    )(log_temp.reshape(1, 1), bias.reshape(1, 1), cotangent.reshape(1, 1), labels.reshape(16, R), img_embed, img_tangent, txt_embed, txt_tangent)
    grads = pl.pallas_call(
        copier, out_shape=[jax.ShapeDtypeStruct((R, D), F32)] * 4, in_specs=[vmem] * 4, out_specs=[anym] * 4,
        scratch_shapes=[dma((4,))],
    )(*[pltpu.with_memory_space_constraint(grad, pltpu.VMEM) for grad in grads])
    grad_img, grad_img_tangent, grad_txt, grad_txt_tangent = grads
    return grad_img, grad_img_tangent, grad_txt, grad_txt_tangent


def solution(mesh):
    rows = P(("img", "txt"), None)
    cols = P(("txt", "img"), None)
    return jax.shard_map(
        body, mesh=mesh,
        in_specs=(rows, rows, cols, cols, P("img"), P(), P(), P()),
        out_specs=(rows, rows, cols, cols), check_vma=False)
```

```python
import functools
import math

import jax
import jax.numpy as jnp
from jax import lax
from jax.experimental import pallas as pl
from jax.experimental.pallas import tpu as pltpu
from jax.sharding import PartitionSpec as P

MESH = pl.DeviceIdType.MESH
F32 = jnp.float32
BF16 = jnp.bfloat16
LOG2E = math.log2(math.e)

ORDER = (7, 4, 6, 5, 2, 3, 1, 0)
EVENTS = (
    ("t", "y6", 5), ("i", "y6", 7), ("t", "c2", 7), ("i", "c2", 8),
    ("t", "y2", 9), ("i", "y2", 10), ("t", "y3", 13), ("i", "y3", 13),
    ("t", "c1", 13), ("i", "c1", 13), ("t", "cb", 13), ("i", "cb", 13),
    ("t", "e1", 13), ("t", "ct", 14), ("i", "e1", 14), ("i", "ct", 15),
)
KEEP0 = (0, 2, 3, 6)
KEEP1 = (0, 1, 2, 5)
TILES = ((0, 0), (0, 1), (1, 0), (1, 1),
         (0, 2), (1, 2), (2, 0), (2, 1), (2, 2),
         (0, 3), (1, 3), (2, 3))


def pick(table, index):
    value = jnp.int32(table[0])
    for at, entry in enumerate(table[1:], 1):
        value = jnp.where(index == at, jnp.int32(entry), value)
    return value


def rows_at(index, size):
    return pl.ds(pl.multiple_of(index * size, size), size)


def split(D):
    return max(1, round(2 * D * 4 / 9 / 128)) * 128


class Copies:
    def __init__(self, send, recv):
        self.send, self.recv, self.table = send, recv, {}

    def add(self, name, src, dst, device):
        at = len(self.table)
        self.table[name] = pltpu.make_async_remote_copy(
            src_ref=src, dst_ref=dst, send_sem=self.send.at[at], recv_sem=self.recv.at[at],
            device_id=device, device_id_type=MESH)

    def start(self, *names):
        for name in names:
            self.table[name].start()

    def landed(self, *names):
        for name in names:
            self.table[name].wait_recv()

    def drain(self):
        for copy in self.table.values():
            copy.wait_send()


N_GATHER = 15 + 15 + 16
N_REDUCE = 17 + 17


def kernel(log_temp_in, bias_in, cotangent_in, labels_in, img_embed, img_tangent, txt_embed, txt_tangent,
           out_img, out_img_tan, out_txt, out_txt_tan,
           im, tx, tan, w, rel, rx_core, rx_i0, rx_i1, rx_t0, rx_t1, keep_i0, keep_i1, keep_t0, keep_t1,
           st_i0, st_i1, st_t0, st_t1, log_temp, bias, cotangent, labels,
           load_sem, g_send, g_recv, r_send, r_recv, c_send, c_recv):
    R, D = txt_embed.shape
    H = R // 2
    S = split(D)
    img, txt = lax.axis_index("img"), lax.axis_index("txt")
    z, y_hi = img // 2, img % 2
    y_lo, x, c = txt // 8, (txt // 2) % 4, txt % 2

    def at_txt(y_lo, x, c):
        return (y_lo * 4 + x) * 2 + c

    core = (img, at_txt(y_lo, x, 1 - c))
    i_y = (img, at_txt(1 - y_lo, x, c))
    i_p, i_m = (img, at_txt(y_lo, (x + 1) % 4, c)), (img, at_txt(y_lo, (x + 3) % 4, c))
    t_y = (z * 2 + 1 - y_hi, at_txt(1 - y_lo, x, c))
    t_p, t_m = (((z + 1) % 4) * 2 + y_hi, txt), (((z + 3) % 4) * 2 + y_hi, txt)

    loads = [
        pltpu.make_async_copy(src, dst, load_sem.at[n])
        for n, (src, dst) in enumerate((
            (img_embed, im.at[0:R, D:2 * D]), (img_tangent, im.at[0:R, 0:D]),
            (txt_embed, tx.at[0:R, 0:D]), (txt_tangent, tan),
            (log_temp_in, log_temp), (bias_in, bias), (cotangent_in, cotangent), (labels_in, labels)))
    ]
    for copy in loads:
        copy.start()
    barrier = pltpu.get_barrier_semaphore()
    peers = (core, i_y, i_p, i_m, t_y, t_p, t_m)
    for peer in peers:
        pl.semaphore_signal(barrier, inc=1, device_id=peer, device_id_type=MESH)
    for copy in loads:
        copy.wait()
    tx[0:R, D:2 * D] = (tx[0:R, 0:D].astype(F32) + tan[...].astype(F32)).astype(BF16)
    pl.semaphore_wait(barrier, len(peers))

    g = Copies(g_send, g_recv)
    families = (("i", im, 2 * R, i_y, i_p, i_m), ("t", tx, R, t_y, t_p, t_m))
    a, b = slice(S, 2 * D), slice(0, S)
    for f, buf, pitch, y, p, m in families:
        def add(name, src, dst, col, to, lo=0, hi=R, f=f, buf=buf, pitch=pitch):
            g.add(f + name, buf.at[src * pitch + lo:src * pitch + hi, col],
                  buf.at[dst * pitch + lo:dst * pitch + hi, col], to)
        add("A1", 0, 1, a, y)
        add("A3", 0, 3, a, p)
        add("A2", 0, 2, a, m)
        add("A5", 1, 5, a, p)
        add("A4", 1, 4, a, m)
        add("A6", 3, 6, a, p)
        add("A7", 4, 7, a, m)
        add("B3", 0, 3, b, p)
        add("B2", 0, 2, b, m)
        add("B6t", 3, 6, b, p, 0, H)
        add("B6b", 2, 6, b, m, H, R)
        add("B1", 0, 1, b, y)
        add("B4", 2, 4, b, y)
        add("B5", 3, 5, b, y)
        add("B7", 6, 7, b, y)
    for k in range(8):
        for name, col in (("A", a), ("B", b)):
            g.add("c%s%d" % (name, k), im.at[2 * R * k:2 * R * k + R, col],
                  im.at[2 * R * k + R:2 * R * (k + 1), col], core)

    def both(*names):
        return [f + name for name in names for f in "it"]

    g.start(*both("A1", "B3", "B2", "A3", "A2", "B1"), "cB0", "cA0")

    lane = lax.broadcasted_iota(jnp.int32, (R, R), 1)

    def place(k, _):
        shift, other = pick((0, 0, 1, 3, 1, 3, 2, 2), k // 2), pick((0, 1, 0, 0, 1, 1, 0, 1), k // 2)
        t = at_txt(jnp.where(other == 1, 1 - y_lo, y_lo), (x + shift) % 4, jnp.where(k % 2 == 1, 1 - c, c))
        row = jnp.broadcast_to(labels[pl.ds(t, 1), :], (R, R))
        rel[rows_at(k, R), :] = row.T - lane
        return 0

    lax.fori_loop(0, 16, place, 0)

    scale = jnp.exp(jnp.broadcast_to(log_temp[...], (1, R)))
    slope, shift = scale * LOG2E, jnp.broadcast_to(bias[...], (1, R)) * LOG2E
    upstream = jnp.broadcast_to(cotangent[...], (1, R))

    def add_up(lo, hi):
        def one(k, _):
            rows = rows_at(k, R)
            im[rows, 2 * D:3 * D] = (im[rows, 0:D].astype(F32) + im[rows, D:2 * D].astype(F32)).astype(BF16)
            return 0
        lax.fori_loop(2 * lo, 2 * hi, one, 0)

    def arrive(slots):
        for k in slots:
            g.landed("cA%d" % k, "cB%d" % k)

    def base_of(k):
        d, other = pick((0, 0, 1, 3, 1, 3, 2, 2), k), pick((0, 1, 0, 0, 1, 1, 0, 1), k)
        hi, lo = jnp.where(other == 1, 1 - y_hi, y_hi), jnp.where(other == 1, 1 - y_lo, y_lo)
        return (at_txt(lo, x, c) * 8 + ((z + d) % 4) * 2 + hi) * R

    def weigh(dots, rows, first, count):
        near = rel[rows, :]
        for n in range(count):
            logit = dots[:, n * R:(n + 1) * R] * slope + shift
            positive = near == base_of(first + n)
            power = jnp.exp2(jnp.where(positive, logit, -logit))
            weight = jnp.where(positive, -upstream, upstream) / (1.0 + power)
            w[rows, rows_at(first + n, R)] = weight.astype(BF16)

    def tile(s, _):
        qp, tp = pick([t[0] for t in TILES], s), pick([t[1] for t in TILES], s)
        rows, cols = rows_at(qp, 4 * R), rows_at(tp, 2 * R)
        dots = lax.dot_general(im[rows, 0:2 * D], tx[cols, :], (((1,), (1,)), ((), ())), preferred_element_type=F32)
        weigh(dots, rows, 2 * tp, 2)
        return 0

    def first():
        g.landed(*both("B3", "B2"))
        g.start(*both("B6t", "B6b", "B5", "B4"), "cB3", "cB2")
        g.landed(*both("A1"))
        g.start(*both("A5", "A4"), "cA1")
        g.landed(*both("B6t", "B6b"))
        g.start(*both("B7"), "cB6")
        g.landed(*both("A3", "A2"))
        g.start(*both("A6"), "cA3", "cA2")
        g.landed(*both("B1"))
        g.start("cB1")
        arrive((0, 1, 2, 3))
        add_up(0, 4)

    def forward():
        g.landed(*both("A4"))
        g.start(*both("A7"), "cA4")

    def second():
        for name in ("B5", "A5", "B4"):
            g.landed("i" + name)
            g.start("c" + name)
        g.landed("tB5", "tA5", "tB4")

    def second_img():
        arrive((4, 5))

    def third():
        add_up(4, 6)
        for name in ("A6", "A7", "B7"):
            g.landed("i" + name)
            g.start("c" + name)
        g.landed("tA6", "tA7", "tB7")

    def third_img():
        arrive((6, 7))

    def part(s, _):
        for at, do in ((0, first), (2, forward), (4, second)):
            @pl.when(s == at)
            def _(do=do):
                do()

        return tile(s, 0)

    lax.fori_loop(0, 6, part, 0)
    second_img()
    rows = pl.ds(8 * R, 4 * R)
    weigh(lax.dot_general(im[rows, 0:2 * D], tx[0:6 * R, :], (((1,), (1,)), ((), ())), preferred_element_type=F32), rows, 0, 6)
    third()
    lax.fori_loop(9, 12, tile, 0)
    third_img()
    rows = pl.ds(12 * R, 4 * R)
    weigh(lax.dot_general(im[rows, 0:2 * D], tx[...], (((1,), (1,)), ((), ())), preferred_element_type=F32), rows, 0, 8)
    add_up(6, 8)
    g.drain()

    r = Copies(r_send, r_recv)
    reduces = (("i", rx_i0, rx_i1, keep_i0, keep_i1, st_i0, st_i1, i_y, i_p, i_m),
               ("t", rx_t0, rx_t1, keep_t0, keep_t1, st_t0, st_t1, t_y, t_p, t_m))
    left, right = ("y0", "y2", "y3", "y6", "pm", "pp", "cc"), ("c1", "f1", "g1", "c2", "f2", "g2", "e1")

    def landing(name, rx0, rx1):
        return rx0.at[left.index(name)] if name in left else rx1.at[right.index(name)]

    for f, rx0, rx1, _, _, s0, s1, y, p, m in reduces:
        def add(name, src, k, to, lo=0, hi=R, into=None, f=f, rx0=rx0, rx1=rx1):
            r.add(f + name, src.at[k, lo:hi], landing(into or name, rx0, rx1).at[lo:hi], to)
        add("c2", s1, 7, m)
        add("y6", s0, 7, y)
        add("c1", s1, 6, p)
        add("g2", s1, 4, p)
        add("y2", s0, 4, y)
        add("g1", s1, 3, m)
        add("y3", s0, 5, y)
        add("y0", s0, 1, y)
        add("ct", s0, 6, p, 0, H, "cc")
        add("cb", s0, 6, m, H, R, "cc")
        add("f2", s1, 5, m)
        add("f1", s1, 2, p)
        add("pmb", s0, 2, p, H, R, "pm")
        add("pmt", s0, 2, p, 0, H, "pm")
        add("ppt", s0, 3, m, 0, H, "pp")
        add("ppb", s0, 3, m, H, R, "pp")
        add("e1", s1, 1, y)

    def core_copy(k):
        return pltpu.make_async_remote_copy(
            src_ref=im.at[rows_at(k, 2 * R), 0:D], dst_ref=rx_core.at[k],
            send_sem=c_send.at[k], recv_sem=c_recv.at[k], device_id=core, device_id_type=MESH)

    def place_of(table, k):
        value = jnp.int32(4)
        for n, entry in enumerate(table):
            value = jnp.where(k == entry, jnp.int32(n), value)
        return value

    def put(k, value, k0, k1, s0, s1):
        value0, value1 = value[:, 0:S], value[:, S:2 * D]
        k0[place_of(KEEP0, k)] = value0
        k1[place_of(KEEP1, k)] = value1
        s0[k] = value0.astype(BF16)
        s1[k] = value1.astype(BF16)

    def send(k, f):
        for slot, names in ((7, ("c2", "y6")), (6, ("c1",)), (4, ("g2", "y2")), (3, ("g1",)), (5, ("y3",)), (1, ("y0",))):
            @pl.when(k == slot)
            def _(names=names):
                r.start(*[f + name for name in names])

    def event(family, do):
        for f, rx0, rx1, k0, k1, s0, s1, *_ in reduces:
            if f == family:
                do(f, lambda name: landing(name, rx0, rx1), k0, k1, s0, s1)

    def after(name, f, rx, k0, k1, s0, s1):
        def got(name, lo=0, hi=R):
            return rx(name)[lo:hi].astype(F32)
        if name == "y6":
            r.landed(f + "y6")
            s0[6] = (k0[KEEP0.index(6)] + got("y6")).astype(BF16)
            r.start(f + "ct", f + "cb")
        elif name == "c2":
            r.landed(f + "c2")
            s1[5] = (k1[KEEP1.index(5)] + got("c2")).astype(BF16)
            r.start(f + "f2")
        elif name == "c1":
            r.landed(f + "c1")
            s1[2] = (k1[KEEP1.index(2)] + got("c1")).astype(BF16)
            r.start(f + "f1")
        elif name == "y2":
            r.landed(f + "y2")
            s0[2, H:R] = (k0[KEEP0.index(2), H:R] + got("y2", H, R)).astype(BF16)
            r.start(f + "pmb")
        elif name == "ct":
            r.landed(f + "ct")
            s0[2, 0:H] = (k0[KEEP0.index(2), 0:H] + got("y2", 0, H) + got("cc", 0, H)).astype(BF16)
            r.start(f + "pmt")
        elif name == "y3":
            r.landed(f + "y3")
            s0[3, 0:H] = (k0[KEEP0.index(3), 0:H] + got("y3", 0, H)).astype(BF16)
            r.start(f + "ppt")
        elif name == "cb":
            r.landed(f + "cb")
            s0[3, H:R] = (k0[KEEP0.index(3), H:R] + got("y3", H, R) + got("cc", H, R)).astype(BF16)
            r.start(f + "ppb")
        elif name == "e1":
            r.landed(f + "g2", f + "f2")
            s1[1] = (k1[KEEP1.index(1)] + got("g2") + got("f2")).astype(BF16)
            r.start(f + "e1")

    def give(k):
        mine, theirs = (pl.ds(pl.multiple_of(k * 2 * R + half, R), R) for half in (0, R))
        part = jnp.dot(w[theirs, :], tx[...], preferred_element_type=F32)
        im[mine, 0:D] = part[:, 0:D].astype(BF16)
        im[theirs, 0:D] = part[:, D:2 * D].astype(BF16)
        core_copy(k).start()

    def follow(n, parity):
        for family, name, at in EVENTS:
            if at < 15 and at % 2 == parity:
                @pl.when(n == at // 2)
                def _(family=family, name=name):
                    event(family, functools.partial(after, name))

    def round_(n, _):
        k = pick(ORDER, n)
        part = lax.dot_general(w[:, rows_at(k, R)], im[:, D:3 * D], (((0,), (0,)), ((), ())), preferred_element_type=F32)
        put(k, part, keep_t0, keep_t1, st_t0, st_t1)
        send(k, "t")
        follow(n, 0)

        @pl.when(n < 7)
        def _():
            give(pick(ORDER, n + 1))

        core_copy(k).wait_recv()
        part = jnp.dot(w[pl.ds(pl.multiple_of(k * 2 * R, R), R), :], tx[...], preferred_element_type=F32)
        part = part + jnp.concatenate([rx_core[k, 0:R], rx_core[k, R:2 * R]], axis=1).astype(F32)
        put(k, part, keep_i0, keep_i1, st_i0, st_i1)
        send(k, "i")
        follow(n, 1)
        return 0

    give(ORDER[0])
    lax.fori_loop(0, 8, round_, 0)
    for family, name, at in EVENTS:
        if at == 15:
            event(family, functools.partial(after, name))

    times = jnp.exp(jnp.broadcast_to(log_temp[...], (1, S)))
    outs = {"i": (out_img_tan, out_img), "t": (out_txt_tan, out_txt)}

    def finish_left(f, rx, k0, k1, s0, s1):
        r.landed(f + "y0", f + "pmb", f + "pmt", f + "ppt", f + "ppb")
        total = k0[0] + rx("y0")[...].astype(F32) + rx("pm")[...].astype(F32) + rx("pp")[...].astype(F32)
        outs[f][0][:, 0:S] = times * total

    def finish_right(f, rx, k0, k1, s0, s1):
        r.landed(f + "f1", f + "g1", f + "e1")
        total = k1[0] + rx("f1")[...].astype(F32) + rx("g1")[...].astype(F32) + rx("e1")[...].astype(F32)
        total = jnp.broadcast_to(times[:, 0:1], total.shape) * total
        outs[f][0][:, S:D] = total[:, 0:D - S]
        outs[f][1][...] = total[:, D - S:]

    event("t", finish_left)
    event("i", finish_left)
    event("t", finish_right)
    event("i", finish_right)
    r.drain()
    for k in range(8):
        core_copy(k).wait_send()


def copier(a, b, c, d, e, f, g, h, sem):
    copies = [pltpu.make_async_copy(src, dst, sem.at[n])
              for n, (src, dst) in enumerate(((a, e), (b, f), (c, g), (d, h)))]
    for copy in copies:
        copy.start()
    for copy in copies:
        copy.wait()


def body(img_embed, img_tangent, txt_embed, txt_tangent, labels, log_temp, bias, cotangent):
    R, D = txt_embed.shape
    S = split(D)
    vmem = pl.BlockSpec(memory_space=pltpu.VMEM)
    anym = pl.BlockSpec(memory_space=pl.ANY)
    out = pltpu.VMEM((R, D), F32)
    dma = pltpu.SemaphoreType.DMA
    grads = pl.pallas_call(
        kernel,
        out_shape=[out] * 4,
        in_specs=[anym] * 8,
        out_specs=[vmem] * 4,
        scratch_shapes=[
            pltpu.VMEM((16 * R, 3 * D), BF16),
            pltpu.VMEM((8 * R, 2 * D), BF16),
            pltpu.VMEM((R, D), BF16),
            pltpu.VMEM((16 * R, 8 * R), BF16),
            pltpu.VMEM((16 * R, R), jnp.int32),
            pltpu.VMEM((8, 2 * R, D), BF16),
        ] + [pltpu.VMEM((7, R, S), BF16), pltpu.VMEM((7, R, 2 * D - S), BF16)] * 2
        + [pltpu.VMEM((5, R, S), F32), pltpu.VMEM((5, R, 2 * D - S), F32)] * 2
        + [pltpu.VMEM((8, R, S), BF16), pltpu.VMEM((8, R, 2 * D - S), BF16)] * 2
        + [pltpu.VMEM((1, 1), F32)] * 3 + [pltpu.VMEM((16, R), jnp.int32)]
        + [dma((8,)), dma((N_GATHER,)), dma((N_GATHER,)), dma((N_REDUCE,)), dma((N_REDUCE,)), dma((8,)), dma((8,))],
        compiler_params=pltpu.CompilerParams(
            collective_id=0, has_side_effects=True, vmem_limit_bytes=60 * 2 ** 20),
    )(log_temp.reshape(1, 1), bias.reshape(1, 1), cotangent.reshape(1, 1), labels.reshape(16, R), img_embed, img_tangent, txt_embed, txt_tangent)
    grads = pl.pallas_call(
        copier, out_shape=[jax.ShapeDtypeStruct((R, D), F32)] * 4, in_specs=[vmem] * 4, out_specs=[anym] * 4,
        scratch_shapes=[dma((4,))],
    )(*[pltpu.with_memory_space_constraint(grad, pltpu.VMEM) for grad in grads])
    grad_img, grad_img_tangent, grad_txt, grad_txt_tangent = grads
    return grad_img, grad_img_tangent, grad_txt, grad_txt_tangent


def solution(mesh):
    rows = P(("img", "txt"), None)
    cols = P(("txt", "img"), None)
    return jax.shard_map(
        body, mesh=mesh,
        in_specs=(rows, rows, cols, cols, P("img"), P(), P(), P()),
        out_specs=(rows, rows, cols, cols), check_vma=False)
```
